256 devices in a mesh: row: 64 (over z, x, core), col: 4 (over y).
Axes of the slice: x: 4, y: 4, z: 8, core: 2. Of those that a mesh axis runs over, the one named last changes fastest.
Arguments:
- off_blocks: bfloat16 [16384, 4, 96, 96], P(('row', 'col')), may hold values from -0.625 to 0.625
- neighbour: int32 [16384, 4], P(('row', 'col')), may hold values from 0 to 5
- active: int32 [16384, 4], P(('row', 'col')), may hold values 0 or 1
- diag_blocks: bfloat16 [16384, 96, 96], P(('row', 'col')), may hold values from -0.625 to 0.625
- diag_inverse: bfloat16 [16384, 96, 96], P(('row', 'col')), may hold values from -0.625 to 0.625
- tentative: bfloat16 [16384, 96, 96], P(('row', 'col')), may hold values from -0.21875 to 0.21875
- aggregate: int32 [16384], P(('row', 'col')), may hold values from 0 to 1
- owner_row: int32 [2048, 1], P('row'), may hold values from 0 to 63; in each aligned block of 32 rows (0 to 31, 32 to 63, ...) at most 2 rows name the same one
- owner_group: int32 [2048], P('row'), may hold values from 0 to 7
Outputs:
- coarse_blocks: float32 [512, 192, 192], P('row', 'col')
The draws below stay inside these ranges and needn't reach their ends.
Inputs may be any that keep to these rules, and one draw needn't show every extreme that they name: `owner_row`: among the 32 clusters of one row tile at most 2 have the same owner row, and exactly 2 do in some tile.
All inputs are finite; a program needn't handle non-finite values. No bound on the sum of `active` on one device may be relied on, other than what follows from the above.
Results may differ from the reference program's by a relative error of at most 0.006.
Values may be sent and summed in bfloat16 or wider, within the bound.
A program may use at most 128 MiB of HBM per device.

```python
import math
import jax
import jax.numpy as jnp
import numpy as np
from jax import lax

B = 96
CW = 2
S = 4
RQ = 2
NQ = 32
G_DEV = 8
CAP = 2
NB = 16384
NQT = 2048
N_ROW = 64
N_COL = 4


def touch_ends(values, key, smallest, top_value):
    shape = values.shape
    index_at = [jax.random.randint(jax.random.fold_in(key, axis), (), 0, shape[axis]) for axis in range(len(shape))]
    values = values.at[tuple(index_at)].set(smallest)
    longest = shape.index(max(shape))
    index_at[longest] = (index_at[longest] + 1) % shape[longest]
    return values.at[tuple(index_at)].set(top_value)


def shard_levels(rng, extent, split, smallest, largest):
    def one(axis_at, shards_of):
        heights = jax.random.uniform(jax.random.fold_in(jax.random.fold_in(rng, 6), axis_at), (shards_of,), jnp.float32, smallest / len(split), largest / len(split))
        return jnp.repeat(jnp.exp(heights), extent[axis_at] // shards_of).reshape((-1,) + (1,) * (len(extent) - axis_at - 1))

    factor_of = one(*split[0])
    for cut in split[1:]:
        factor_of = factor_of * one(*cut)
    return factor_of


def shared_out(rng, own, number, rows, count, top, most, skew):
    order = jax.random.permutation(rng, count)
    heavy_load, usual = portions_of(count, rows * top, most, skew, True), portions_of(count, rows * top, most, skew, False)
    places = jnp.arange(count)

    def named(lengths, offset_by):
        used = int((lengths > 0).sum())
        fixed = max(1, used // 4)
        shifted = fixed + (places - fixed + offset_by * (used - fixed)) % max(1, count - fixed)
        return jnp.zeros((count,), jnp.int32).at[order[jnp.where(places < fixed, places, shifted)]].set(jnp.asarray(lengths, jnp.int32))

    lengths = jnp.where(number % 4 == 0, named(heavy_load, number // 4), named(usual, number - number // 4 - 1))
    mixed = jax.random.permutation(jax.random.fold_in(own, 3), count)
    giver, receiver = mixed[0:count // 2 * 2:2], mixed[1:count // 2 * 2:2]
    margin = jnp.minimum(lengths[giver] - 1, most - lengths[receiver]) // 2
    margin = jnp.where((giver == order[0]) | (receiver == order[0]) | (lengths[receiver] == 0), 0, jnp.maximum(margin, 0))
    shifted = jax.random.randint(jax.random.fold_in(own, 4), (count // 2,), 0, 1 << 20) % (margin + 1)
    lengths = lengths.at[giver].add(-shifted).at[receiver].add(shifted)
    items = jnp.searchsorted(jnp.cumsum(lengths), jnp.arange(rows * top), side="right").astype(jnp.int32)
    table = items.reshape(top, rows).T
    table = table[jax.random.permutation(jax.random.fold_in(own, 1), rows)]
    offset_by = jax.random.randint(jax.random.fold_in(own, 2), (rows, 1), 0, top)
    return jnp.take_along_axis(table, (jnp.arange(top)[None, :] + offset_by) % top, axis=1)


def portions_of(number_of, total, limit, lean, full):
    weights = [(1 << 20) // math.isqrt(grade ** lean) + 1 for grade in range(1, number_of + 1)]
    largest = limit if full else min(limit, max(-(-total // number_of), total * weights[0] // sum(weights)))
    least = 1 if total - largest >= number_of - 1 else 0
    counts, spare = [largest] + [least] * (number_of - 1), total - largest - least * (number_of - 1)
    while spare > 0:
        movable = [i for i in range(1, number_of) if counts[i] < largest] or [i for i in range(1, number_of) if counts[i] < limit]
        mass, budget = sum([weights[i] for i in movable]), spare
        for i in movable:
            extra = min(limit - counts[i], max(1, budget * weights[i] // mass), spare)
            counts[i] = counts[i] + extra
            spare = spare - extra
    return np.array(counts)


def centred(rng, dims, deviation, limit, shards=(), kind=jnp.bfloat16):
    array = jax.random.normal(rng, dims, jnp.float32) * deviation
    if len(shards) > 0:
        array = shard_levels(rng, dims, shards, -0.22, 0.18) * array
    return jnp.clip(array, min=-limit, max=limit).astype(kind)


def setup_inputs(seed: int = 0) -> dict:
    splits = jax.random.split(jax.random.key(seed), 10)
    off_blocks = centred(splits[0], (NB, S, B, B), B ** -0.5, 0.625, ((0, 256),))
    neighbour = touch_ends(jax.random.randint(splits[1], (NB, S), 0, 3 * RQ), jax.random.fold_in(splits[1], 1), 0, (3 * RQ) - 1).astype(jnp.int32)
    active = touch_ends((jax.random.randint(splits[2], (NB, S), 0, 20) < 19).astype(jnp.int32), jax.random.fold_in(splits[2], 1), 0, 1)
    diag_blocks = centred(splits[3], (NB, B, B), B ** -0.5, 0.625, ((0, 256),))
    diag_inverse = centred(splits[4], (NB, B, B), B ** -0.5, 0.625, ((0, 256),))
    tentative = centred(splits[5], (NB, B, B), (8 * B) ** -0.5, 0.21875, ((0, 256),))
    aggregate = touch_ends(jax.random.randint(splits[6], (NB,), 0, CW), jax.random.fold_in(splits[6], 1), 0, CW - 1).astype(jnp.int32)
    owner_row_keys = jax.random.split(jax.random.fold_in(splits[7], 1), NQT // NQ)
    owner_row_turns = jax.random.permutation(jax.random.fold_in(splits[7], 3), NQT // NQ)
    owner_row = jax.vmap(lambda own, number: shared_out(jax.random.fold_in(splits[7], 2), own, number, NQ, N_ROW, 1, CAP, 2))(owner_row_keys, owner_row_turns).reshape((NQT, 1))
    owner_group = touch_ends(jax.random.randint(splits[8], (NQT,), 0, G_DEV), jax.random.fold_in(splits[8], 1), 0, G_DEV - 1).astype(jnp.int32)
    return dict(off_blocks=off_blocks, neighbour=neighbour, active=active, diag_blocks=diag_blocks, diag_inverse=diag_inverse, tentative=tentative, aggregate=aggregate, owner_row=owner_row, owner_group=owner_group)


OMEGA = 0.6


def widen(blocks, labels, window):
    onehot = (labels[..., None] == jnp.arange(window, dtype=jnp.int32)).astype(blocks.dtype)
    spread_out = blocks[..., :, None, :] * onehot[..., None, :, None]
    return spread_out.reshape(blocks.shape[:-1] + (window * blocks.shape[-1],))


def neighbour_index(near_slots, per_device):
    row_count = near_slots.shape[0]
    cluster_base = (jnp.arange(row_count, dtype=jnp.int32) // per_device) * per_device
    return ((near_slots // per_device) * row_count + cluster_base[:, None] + near_slots % per_device).astype(jnp.int32)


def apply_rows(diag_part, off_part, active_part, with_rim, near_index):
    row_count = diag_part.shape[0]
    own_rows = with_rim[row_count:2 * row_count].astype(jnp.float32)
    near_rows = jnp.take(with_rim, near_index, axis=0).astype(jnp.float32)
    weights = off_part.astype(jnp.float32) * active_part[:, :, None, None].astype(jnp.float32)
    summed = jnp.einsum('rij,rjw->riw', diag_part.astype(jnp.float32), own_rows)
    return summed + jnp.einsum('rsij,rsjw->riw', weights, near_rows)


def add_rim(field):
    return jnp.concatenate([jnp.roll(field, 1, axis=0), field, jnp.roll(field, -1, axis=0)], axis=1)


def tile_blocks(tile_arrays):
    off_t, near_t, active_t, diag_t, inverse_t, tent_t, aggregate_t = tile_arrays
    near_index = jax.vmap(lambda slots: neighbour_index(slots, RQ))(near_t)
    tent_wide = widen(tent_t, aggregate_t, CW)
    smooth_in = jax.vmap(apply_rows)(diag_t, off_t, active_t, add_rim(tent_wide), near_index).astype(jnp.bfloat16)
    correction = jnp.einsum('crij,crjw->criw', inverse_t.astype(jnp.float32), smooth_in.astype(jnp.float32))
    prolong = (tent_wide.astype(jnp.float32) - OMEGA * correction).astype(jnp.bfloat16)
    stiff_prol = jax.vmap(apply_rows)(diag_t, off_t, active_t, add_rim(prolong), near_index).astype(jnp.bfloat16)
    window = CW * B
    left_side = prolong.reshape(N_COL, NQ, RQ * B, window).transpose(1, 0, 2, 3).reshape(NQ, N_COL * RQ * B, window)
    right_side = stiff_prol.reshape(N_COL, NQ, RQ * B, window).transpose(1, 0, 2, 3).reshape(NQ, N_COL * RQ * B, window)
    return jnp.einsum('qmx,qmy->qxy', left_side.astype(jnp.float32), right_side.astype(jnp.float32))


def reference(off_blocks, neighbour, active, diag_blocks, diag_inverse, tentative, aggregate, owner_row, owner_group):
    def by_tiles(values):
        return values.reshape((N_ROW, N_COL, NQ * RQ) + values.shape[1:])

    tile_arrays = tuple(by_tiles(values) for values in (off_blocks, neighbour, active, diag_blocks, diag_inverse, tentative, aggregate))
    blocks = lax.map(tile_blocks, tile_arrays)
    blocks = blocks.reshape(N_ROW * NQ, CW * B, CW * B)
    target = (owner_row[:, 0] * G_DEV + owner_group).astype(jnp.int32)
    return jax.ops.segment_sum(blocks, target, num_segments=N_ROW * G_DEV)
```

```python
import jax
import jax.numpy as jnp
from jax import lax
from jax.experimental import pallas as pl
from jax.experimental.pallas import tpu as pltpu
from jax.sharding import PartitionSpec as P

MESH = pl.DeviceIdType.MESH
F32 = jnp.float32
BF16 = jnp.bfloat16
B = 96
LANES = 128
OMEGA = 0.6
ROWS = 64
PAIRS = 16
PEERS = 64
PLANES = 48


def pack4(b0, b1, b2, b3):
    high = lax.broadcasted_iota(jnp.int32, b0.shape, 1) >= B
    return (
        jnp.where(high, pltpu.roll(b3, 96, 1), b0),
        jnp.where(high, pltpu.roll(b3, 64, 1), b1),
        jnp.where(high, pltpu.roll(b3, 32, 1), b2),
    )


def unpack_last(t0, t1, t2):
    lane = lax.broadcasted_iota(jnp.int32, t0.shape, 1)
    return jnp.where(
        lane < 32,
        pltpu.roll(t0, 32, 1),
        jnp.where(lane < 64, pltpu.roll(t1, 64, 1), pltpu.roll(t2, 96, 1)),
    )


def dot(a, b):
    return lax.dot_general(a, b, (((1,), (0,)), ((), ())), preferred_element_type=F32)


def galerkin_kernel(
    slot_ref,
    label_ref,
    off_hbm,
    diag_hbm,
    inv_hbm,
    tent_hbm,
    out_ref,
    off,
    diag,
    inv,
    tent,
    wide,
    send_label,
    near_label,
    send_t,
    near_t,
    own_p,
    send_p,
    near_p,
    rim,
    part,
    send_far,
    send_next,
    send_back,
    near_far,
    near_next,
    near_back,
    hold_next,
    hold_own,
    planes,
    load_sem,
    tent_sem,
    label_send,
    label_recv,
    t_send,
    t_recv,
    p_send,
    p_recv,
    c_send,
    c_recv,
):
    me = lax.axis_index("col")
    right, left = lax.rem(me + 1, 4), lax.rem(me + 3, 4)

    def loads(p):
        rows = pl.ds(p * 4, 4)
        return [
            pltpu.make_async_copy(off_hbm.at[rows], off.at[rows], load_sem.at[0, p]),
            pltpu.make_async_copy(diag_hbm.at[rows], diag.at[rows], load_sem.at[1, p]),
            pltpu.make_async_copy(inv_hbm.at[rows], inv.at[rows], load_sem.at[2, p]),
        ]

    def remote(src, dst, send_sem, recv_sem, col):
        return pltpu.make_async_remote_copy(
            src_ref=src,
            dst_ref=dst,
            send_sem=send_sem,
            recv_sem=recv_sem,
            device_id={"col": col},
            device_id_type=MESH,
        )

    tent_copy = pltpu.make_async_copy(tent_hbm, tent, tent_sem)
    tent_copy.start()

    @pl.loop(0, PAIRS)
    def _(p):
        for copy in loads(p):
            copy.start()

    barrier = pltpu.get_barrier_semaphore()
    for peer in (left, right):
        pl.semaphore_signal(barrier, inc=1, device_id={"col": peer}, device_id_type=MESH)
    send_label[...] = label_ref[...]
    rim[...] = jnp.zeros_like(rim)
    pl.semaphore_wait(barrier, 2)

    def label_copy(side):
        return remote(
            send_label, near_label.at[side], label_send.at[side], label_recv.at[side],
            right if side == 0 else left,
        )

    def t_copy(side, p):
        return remote(
            send_t.at[p], near_t.at[side, p], t_send.at[side, p], t_recv.at[side, p],
            right if side == 0 else left,
        )

    def p_copy(side, p):
        rows = pl.ds(p * 2, 2)
        return remote(
            send_p.at[rows], near_p.at[side, rows], p_send.at[side, p], p_recv.at[side, p],
            right if side == 0 else left,
        )

    for side in range(2):
        label_copy(side).start()
    tent_copy.wait()

    @pl.loop(0, PAIRS)
    def _(p):
        for e in range(4):
            wide[p * 4 + e, :, 0:B] = tent[p * 4 + e]
        tiles = pack4(*[wide[p * 4 + e].astype(F32) for e in range(4)])
        for t in range(3):
            send_t[p, t] = tiles[t].astype(BF16)
        for side in range(2):
            t_copy(side, p).start()

    for side in range(2):
        label_copy(side).wait_recv()

    def apply(row, near_base, own):
        total = dot(diag[row], rim[near_base + own])
        for s in range(4):
            total = total + dot(off[row, s], rim[near_base + slot_ref[row * 4 + s]])
        return total

    @pl.loop(0, PAIRS)
    def _(p):
        for side in range(2):
            t_copy(side, p).wait_recv()
        for copy in loads(p):
            copy.wait()

        def spread(e, position, block, label):
            zero = jnp.zeros_like(block)
            at = (e // 2) * 7 + position + e % 2
            rim[at, :, 0:LANES] = jnp.where(label == 0.0, block, zero).astype(BF16)
            rim[at, :, LANES : 2 * LANES] = jnp.where(label == 1.0, block, zero).astype(BF16)

        for side in range(2):
            tiles = [near_t[side, p, t].astype(F32) for t in range(3)]
            tiles.append(unpack_last(*tiles))
            for e in range(4):
                spread(e, 4 * side, tiles[e], near_label[side, pl.ds(p * 4 + e, 1), :])
        for e in range(4):
            spread(e, 2, wide[p * 4 + e].astype(F32), send_label[pl.ds(p * 4 + e, 1), :])

        for c in range(2):
            blocks = []
            for k in range(2):
                row = p * 4 + c * 2 + k
                smooth = apply(row, c * 7, 2 + k).astype(BF16)
                prolong = rim[c * 7 + 2 + k].astype(F32) - OMEGA * dot(inv[row], smooth)
                rounded = prolong.astype(BF16)
                own_p[row] = rounded
                back = rounded.astype(F32)
                blocks += [back[:, 0:LANES], back[:, LANES : 2 * LANES]]
            tiles = pack4(*blocks)
            for t in range(3):
                send_p[p * 2 + c, t] = tiles[t].astype(BF16)
        for side in range(2):
            p_copy(side, p).start()

    def ways(p):
        odd = lax.rem(p, 2)
        ahead = lax.rem(me + 3 + 2 * odd, 4)
        behind = lax.rem(me + 1 + 2 * odd, 4)
        return ahead, behind

    def far_copy(p):
        return remote(
            send_far.at[p], near_far.at[p], c_send.at[0, p], c_recv.at[0, p], ways(p)[0]
        )

    def next_copy(p):
        return remote(
            send_next.at[p], near_next.at[p], c_send.at[1, p], c_recv.at[1, p], ways(p)[0]
        )

    def back_copy(p):
        return remote(
            send_back.at[p], near_back.at[p], c_send.at[2, p], c_recv.at[2, p], ways(p)[1]
        )

    def forward(p):
        far_copy(p).wait_recv()
        for t in range(3):
            send_next[p, t] = (hold_next[p, t] + near_far[p, t].astype(F32)).astype(BF16)
        next_copy(p).start()

    def finish(p):
        next_copy(p).wait_recv()
        back_copy(p).wait_recv()
        for t in range(3):
            planes[t, pl.ds(p, PLANES, stride=PAIRS), :] = (
                hold_own[p, t] + near_next[p, t].astype(F32) + near_back[p, t].astype(F32)
            )

    @pl.loop(0, PAIRS)
    def _(p):
        for side in range(2):
            p_copy(side, p).wait_recv()
        for c in range(2):
            for side in range(2):
                tiles = [near_p[side, p * 2 + c, t] for t in range(3)]
                last = unpack_last(*[tile.astype(F32) for tile in tiles]).astype(BF16)
                tiles.append(last)
                for e in range(4):
                    lanes = slice((e % 2) * LANES, (e % 2 + 1) * LANES)
                    rim[c * 7 + 4 * side + e // 2, :, lanes] = tiles[e]
            for k in range(2):
                rim[c * 7 + 2 + k] = own_p[p * 4 + c * 2 + k]
            total = None
            for k in range(2):
                row = p * 4 + c * 2 + k
                stiff = apply(row, c * 7, 2 + k).astype(BF16)
                term = lax.dot_general(
                    rim[c * 7 + 2 + k], stiff, (((0,), (0,)), ((), ())),
                    preferred_element_type=F32,
                )
                total = term if total is None else total + term
            part[c] = total

        def share(col):
            start = pl.multiple_of((col // 2) * LANES + lax.rem(col, 2) * 48, 16)
            rows = pl.ds(start, 48)
            return pack4(
                part[0, rows, 0:LANES],
                part[0, rows, LANES : 2 * LANES],
                part[1, rows, 0:LANES],
                part[1, rows, LANES : 2 * LANES],
            )

        ahead, behind = ways(p)
        tiles = share(lax.rem(me + 2, 4))
        for t in range(3):
            send_far[p, t] = tiles[t].astype(BF16)
        far_copy(p).start()
        tiles = share(behind)
        for t in range(3):
            send_back[p, t] = tiles[t].astype(BF16)
        back_copy(p).start()
        tiles = share(ahead)
        for t in range(3):
            hold_next[p, t] = tiles[t]
        tiles = share(me)
        for t in range(3):
            hold_own[p, t] = tiles[t]

        @pl.when(p >= 1)
        def _():
            forward(p - 1)

        @pl.when(p >= 2)
        def _():
            finish(p - 2)

    forward(PAIRS - 1)
    finish(PAIRS - 2)
    finish(PAIRS - 1)

    @pl.loop(0, PLANES)
    def _(r):
        for t in range(3):
            rows = pl.ds(pl.multiple_of(r * PAIRS, PAIRS), PAIRS)
            out_ref[r, t] = planes[t, rows, :].astype(BF16)

    for side in range(2):
        label_copy(side).wait_send()

    @pl.loop(0, PAIRS)
    def _(p):
        for side in range(2):
            t_copy(side, p).wait_send()
            p_copy(side, p).wait_send()
        far_copy(p).wait_send()
        next_copy(p).wait_send()
        back_copy(p).wait_send()


def galerkin(slots, labels, off, diag, inv, tent):
    dma = pltpu.SemaphoreType.DMA
    hbm = pl.BlockSpec(memory_space=pl.ANY)
    return pl.pallas_call(
        galerkin_kernel,
        out_shape=jax.ShapeDtypeStruct((PLANES, 3, PAIRS, LANES), BF16),
        in_specs=[
            pl.BlockSpec(memory_space=pltpu.SMEM),
            pl.BlockSpec(memory_space=pltpu.VMEM),
            hbm,
            hbm,
            hbm,
            hbm,
        ],
        out_specs=pl.BlockSpec(memory_space=pltpu.VMEM),
        scratch_shapes=[
            pltpu.VMEM((ROWS, 4, B, B), BF16),
            pltpu.VMEM((ROWS, B, B), BF16),
            pltpu.VMEM((ROWS, B, B), BF16),
            pltpu.VMEM((ROWS, B, B), BF16),
            pltpu.VMEM((ROWS, B, LANES), BF16),
            pltpu.VMEM((ROWS, LANES), F32),
            pltpu.VMEM((2, ROWS, LANES), F32),
            pltpu.VMEM((PAIRS, 3, B, LANES), BF16),
            pltpu.VMEM((2, PAIRS, 3, B, LANES), BF16),
            pltpu.VMEM((ROWS, B, 2 * LANES), BF16),
            pltpu.VMEM((2 * PAIRS, 3, B, LANES), BF16),
            pltpu.VMEM((2, 2 * PAIRS, 3, B, LANES), BF16),
            pltpu.VMEM((14, B, 2 * LANES), BF16),
            pltpu.VMEM((2, 2 * LANES, 2 * LANES), F32),
            pltpu.VMEM((PAIRS, 3, 48, LANES), BF16),
            pltpu.VMEM((PAIRS, 3, 48, LANES), BF16),
            pltpu.VMEM((PAIRS, 3, 48, LANES), BF16),
            pltpu.VMEM((PAIRS, 3, 48, LANES), BF16),
            pltpu.VMEM((PAIRS, 3, 48, LANES), BF16),
            pltpu.VMEM((PAIRS, 3, 48, LANES), BF16),
            pltpu.VMEM((PAIRS, 3, 48, LANES), F32),
            pltpu.VMEM((PAIRS, 3, 48, LANES), F32),
            pltpu.VMEM((3, PLANES * PAIRS, LANES), F32),
            dma((3, PAIRS)),
            dma,
            dma((2,)),
            dma((2,)),
            dma((2, PAIRS)),
            dma((2, PAIRS)),
            dma((2, PAIRS)),
            dma((2, PAIRS)),
            dma((3, PAIRS)),
            dma((3, PAIRS)),
        ],
        compiler_params=pltpu.CompilerParams(
            collective_id=0, has_side_effects=True, vmem_limit_bytes=52 * 1024 * 1024
        ),
    )(slots, labels, off, diag, inv, tent)


def plane_device(r):
    z = r // 6
    return z * 8 + lax.rem(lax.rem(r, 6) + 2 * z + 2, 8)


def owner_kernel(planes_ref, target_ref, out_ref, gathered, sums, send, landed, wide, sems):
    me = lax.axis_index("row")
    z = me // 8
    place = lax.rem(lax.rem(me, 8) + 32 - 2 * z - 2, 8)
    holds = place < 6
    plane = z * 6 + place

    def plane_copy(r, target):
        return pltpu.make_async_remote_copy(
            src_ref=planes_ref.at[r],
            dst_ref=gathered.at[me],
            send_sem=sems.at[0],
            recv_sem=sems.at[1],
            device_id={"row": target},
            device_id_type=MESH,
        )

    def group_copy(target):
        return pltpu.make_async_remote_copy(
            src_ref=send.at[target],
            dst_ref=landed.at[plane],
            send_sem=sems.at[2],
            recv_sem=sems.at[3],
            device_id={"row": target},
            device_id_type=MESH,
        )

    barrier = pltpu.get_barrier_semaphore()

    @pl.loop(1, PEERS)
    def _(d):
        pl.semaphore_signal(
            barrier, inc=1, device_id={"row": lax.rem(me + d, PEERS)}, device_id_type=MESH
        )

    pl.semaphore_wait(barrier, PEERS - 1)

    @pl.loop(0, PLANES)
    def _(d):
        r = lax.rem(z * 6 + d, PLANES)
        target = plane_device(r)

        @pl.when(target != me)
        def _():
            plane_copy(r, target).start()

        @pl.when(target == me)
        def _():
            pltpu.make_async_copy(planes_ref.at[r], gathered.at[me], sems.at[1]).start()

    @pl.when(holds)
    def _():
        pltpu.make_async_copy(gathered, gathered, sems.at[1]).wait()
        tiles = [
            gathered[:, t].astype(F32).reshape(PEERS * PAIRS, LANES) for t in range(3)
        ]
        tiles.append(unpack_last(*tiles))
        tiles = [tile.astype(BF16) for tile in tiles]
        group = lax.broadcasted_iota(jnp.int32, (8 * PEERS, PEERS * PAIRS), 0)
        first = jnp.where(group == target_ref[0:1, :], 1.0, 0.0).astype(BF16)
        second = jnp.where(group == target_ref[1:2, :], 1.0, 0.0).astype(BF16)
        for c in range(2):
            total = dot(first, tiles[c]) + dot(second, tiles[2 + c])
            sums[:, c * 8 : (c + 1) * 8, :] = total.reshape(PEERS, 8, LANES)
        send[...] = sums[...].astype(BF16)

        @pl.loop(0, PEERS)
        def _(d):
            target = lax.rem(me + d, PEERS)

            @pl.when(target != me)
            def _():
                group_copy(target).start()

            @pl.when(target == me)
            def _():
                pltpu.make_async_copy(send.at[me], landed.at[plane], sems.at[3]).start()

    pltpu.make_async_copy(landed, landed, sems.at[3]).wait()
    wide[...] = landed[...].astype(F32).reshape(PLANES * 16, LANES)
    for g in range(8):
        first = wide[pl.ds(g, PLANES, stride=16), :]
        second = pltpu.roll(wide[pl.ds(8 + g, PLANES, stride=16), :], 96, 1)
        high = lax.broadcasted_iota(jnp.int32, first.shape, 1) >= B
        out_ref[g, :, 0:LANES] = jnp.where(high, second, first)
        out_ref[g, :, LANES : 2 * B] = second[:, 0 : 2 * B - LANES]

    @pl.loop(0, PLANES)
    def _(r):
        target = plane_device(r)

        @pl.when(target != me)
        def _():
            plane_copy(r, target).wait_send()

    @pl.when(holds)
    def _():
        @pl.loop(1, PEERS)
        def _(d):
            group_copy(lax.rem(me + d, PEERS)).wait_send()


def to_owners(planes, targets):
    vmem = pl.BlockSpec(memory_space=pltpu.VMEM)
    return pl.pallas_call(
        owner_kernel,
        out_shape=jax.ShapeDtypeStruct((8, PLANES, 2 * B), F32),
        in_specs=[vmem, vmem],
        out_specs=vmem,
        scratch_shapes=[
            pltpu.VMEM((PEERS, 3, PAIRS, LANES), BF16),
            pltpu.VMEM((PEERS, 16, LANES), F32),
            pltpu.VMEM((PEERS, 16, LANES), BF16),
            pltpu.VMEM((PLANES, 16, LANES), BF16),
            pltpu.VMEM((PLANES * 16, LANES), F32),
            pltpu.SemaphoreType.DMA((4,)),
        ],
        compiler_params=pltpu.CompilerParams(
            collective_id=1, has_side_effects=True, vmem_limit_bytes=32 * 1024 * 1024
        ),
    )(planes, targets)


def on_device(
    off_blocks,
    neighbour,
    active,
    diag_blocks,
    diag_inverse,
    tentative,
    aggregate,
    owner_row,
    owner_group,
):
    target = owner_row[:, 0] * 8 + owner_group
    targets = lax.all_gather(target, "row")
    targets = targets.reshape(PEERS * PAIRS, 2).T
    slots = jnp.where(active != 0, neighbour, 6).reshape(-1)
    labels = jnp.broadcast_to(aggregate.astype(F32)[:, None], (ROWS, LANES))
    planes = galerkin(slots, labels, off_blocks, diag_blocks, diag_inverse, tentative)
    return to_owners(planes, targets)


def solution(mesh):
    return jax.shard_map(
        on_device,
        mesh=mesh,
        in_specs=(
            P(("row", "col"), None, None, None),
            P(("row", "col"), None),
            P(("row", "col"), None),
            P(("row", "col"), None, None),
            P(("row", "col"), None, None),
            P(("row", "col"), None, None),
            P(("row", "col")),
            P("row", None),
            P("row"),
        ),
        out_specs=P("row", "col", None),
        check_vma=False,
    )
```

```python
import jax
import jax.numpy as jnp
from jax import lax
from jax.experimental import pallas as pl
from jax.experimental.pallas import tpu as pltpu
from jax.sharding import PartitionSpec as P

MESH = pl.DeviceIdType.MESH
F32 = jnp.float32
BF16 = jnp.bfloat16
B = 96
LANES = 128
OMEGA = 0.6
ROWS = 64
PAIRS = 16
PEERS = 64
PLANES = 48
CHUNKS = 4
WINDOW = 3
LAG = 3


def pack4(b0, b1, b2, b3):
    high = lax.broadcasted_iota(jnp.int32, b0.shape, 1) >= B
    return (
        jnp.where(high, pltpu.roll(b3, 96, 1), b0),
        jnp.where(high, pltpu.roll(b3, 64, 1), b1),
        jnp.where(high, pltpu.roll(b3, 32, 1), b2),
    )


def unpack_last(t0, t1, t2):
    lane = lax.broadcasted_iota(jnp.int32, t0.shape, 1)
    return jnp.where(
        lane < 32,
        pltpu.roll(t0, 32, 1),
        jnp.where(lane < 64, pltpu.roll(t1, 64, 1), pltpu.roll(t2, 96, 1)),
    )


def dot(a, b):
    return lax.dot_general(a, b, (((1,), (0,)), ((), ())), preferred_element_type=F32)


def plane_device(r):
    z = r // 6
    return z * 8 + lax.rem(lax.rem(r, 6) + 2 * z + 2, 8)


def galerkin_kernel(
    near_smem,
    active_smem,
    label_smem,
    owner_smem,
    group_smem,
    off_hbm,
    diag_hbm,
    inv_hbm,
    tent_hbm,
    out_ref,
    off,
    diag,
    inv,
    tent,
    wide,
    send_label,
    near_label,
    send_t,
    near_t,
    own_p,
    send_p,
    near_p,
    rim,
    part,
    send_far,
    send_next,
    send_back,
    near_far,
    near_next,
    near_back,
    hold_next,
    hold_own,
    staging,
    send_target,
    near_target,
    onehot,
    send_plane,
    near_plane,
    total_sum,
    send_group,
    near_group,
    final,
    load_sem,
    tent_sem,
    label_send,
    label_recv,
    t_send,
    t_recv,
    p_send,
    p_recv,
    c_send,
    c_recv,
    target_sem,
    plane_send,
    plane_recv,
    group_sem,
):
    me = lax.axis_index("col")
    right, left = lax.rem(me + 1, 4), lax.rem(me + 3, 4)
    tile = lax.axis_index("row")
    z = tile // 8
    place = lax.rem(lax.rem(tile, 8) + 32 - 2 * z - 2, 8)
    holds = place < 6
    plane = z * 6 + place

    def loads(p):
        rows = pl.ds(p * 4, 4)
        return [
            pltpu.make_async_copy(off_hbm.at[rows], off.at[rows], load_sem.at[0, p]),
            pltpu.make_async_copy(diag_hbm.at[rows], diag.at[rows], load_sem.at[1, p]),
            pltpu.make_async_copy(inv_hbm.at[rows], inv.at[rows], load_sem.at[2, p]),
        ]

    def remote(src, dst, send_sem, recv_sem, col):
        return pltpu.make_async_remote_copy(
            src_ref=src,
            dst_ref=dst,
            send_sem=send_sem,
            recv_sem=recv_sem,
            device_id={"col": col},
            device_id_type=MESH,
        )

    def along_row(src, dst, send_sem, recv_sem, target):
        return pltpu.make_async_remote_copy(
            src_ref=src,
            dst_ref=dst,
            send_sem=send_sem,
            recv_sem=recv_sem,
            device_id={"row": target},
            device_id_type=MESH,
        )

    tent_copy = pltpu.make_async_copy(tent_hbm, tent, tent_sem)
    tent_copy.start()

    barrier = pltpu.get_barrier_semaphore()
    for peer in (left, right):
        pl.semaphore_signal(barrier, inc=1, device_id={"col": peer}, device_id_type=MESH)

    @pl.loop(1, PEERS)
    def _(d):
        pl.semaphore_signal(
            barrier, inc=1, device_id={"row": lax.rem(tile + d, PEERS)}, device_id_type=MESH
        )

    @pl.loop(0, PAIRS)
    def _(p):
        for copy in loads(p):
            copy.start()

    rim[6] = jnp.zeros_like(rim[6])
    rim[13] = jnp.zeros_like(rim[13])

    @pl.loop(0, ROWS)
    def _(f):
        send_label[pl.ds(f, 1), :] = jnp.full((1, LANES), label_smem[f], jnp.int32).astype(F32)

    sub = lax.broadcasted_iota(jnp.int32, (8, LANES), 0)
    lane = lax.broadcasted_iota(jnp.int32, (8, LANES), 1)
    mine = jnp.zeros((8, LANES), jnp.int32)
    for q in range(32):
        here = (sub == q // 8) & (lane == lax.rem(tile, 16) * 8 + q % 8)
        mine = jnp.where(here, owner_smem[q] * 8 + group_smem[q], mine)
    send_target[...] = mine

    tent_copy.wait()

    @pl.loop(0, PAIRS)
    def _(p):
        for e in range(4):
            wide[p * 4 + e, :, 0:B] = tent[p * 4 + e]
        tiles = pack4(*[wide[p * 4 + e].astype(F32) for e in range(4)])
        for t in range(3):
            send_t[p, t] = tiles[t].astype(BF16)

    pl.semaphore_wait(barrier, PEERS + 1)

    def label_copy(side):
        return remote(
            send_label, near_label.at[side], label_send.at[side], label_recv.at[side],
            right if side == 0 else left,
        )

    def t_copy(side, p):
        return remote(
            send_t.at[p], near_t.at[side, p], t_send.at[side, p], t_recv.at[side, p],
            right if side == 0 else left,
        )

    def p_copy(side, p):
        rows = pl.ds(p * 2, 2)
        return remote(
            send_p.at[rows], near_p.at[side, rows], p_send.at[side, p], p_recv.at[side, p],
            right if side == 0 else left,
        )

    def target_copy(target):
        return along_row(
            send_target, near_target.at[tile], target_sem.at[0], target_sem.at[1], target
        )

    for side in range(2):
        label_copy(side).start()

    @pl.loop(0, PAIRS)
    def _(p):
        for side in range(2):
            t_copy(side, p).start()

    @pl.loop(0, PLANES)
    def _(r):
        target = plane_device(r)

        @pl.when(target != tile)
        def _():
            target_copy(target).start()

    @pl.when(holds)
    def _():
        pltpu.make_async_copy(send_target, near_target.at[tile], target_sem.at[1]).start()

    for side in range(2):
        label_copy(side).wait_recv()

    def apply(row, near_base, own):
        total = dot(diag[row], rim[near_base + own])
        for s in range(4):
            on = active_smem[s, row]
            slot = near_smem[s, row] * on + 6 * (1 - on)
            total = total + dot(off[row, s], rim[near_base + slot])
        return total

    @pl.loop(0, PAIRS)
    def _(p):
        for side in range(2):
            t_copy(side, p).wait_recv()
        for copy in loads(p):
            copy.wait()

        def spread(e, position, block, label):
            zero = jnp.zeros_like(block)
            at = (e // 2) * 7 + position + e % 2
            rim[at, :, 0:LANES] = jnp.where(label == 0.0, block, zero).astype(BF16)
            rim[at, :, LANES : 2 * LANES] = jnp.where(label == 1.0, block, zero).astype(BF16)

        for side in range(2):
            tiles = [near_t[side, p, t].astype(F32) for t in range(3)]
            tiles.append(unpack_last(*tiles))
            for e in range(4):
                spread(e, 4 * side, tiles[e], near_label[side, pl.ds(p * 4 + e, 1), :])
        for e in range(4):
            spread(e, 2, wide[p * 4 + e].astype(F32), send_label[pl.ds(p * 4 + e, 1), :])

        for c in range(2):
            blocks = []
            for k in range(2):
                row = p * 4 + c * 2 + k
                smooth = apply(row, c * 7, 2 + k).astype(BF16)
                prolong = rim[c * 7 + 2 + k].astype(F32) - OMEGA * dot(inv[row], smooth)
                rounded = prolong.astype(BF16)
                own_p[row] = rounded
                back = rounded.astype(F32)
                blocks += [back[:, 0:LANES], back[:, LANES : 2 * LANES]]
            tiles = pack4(*blocks)
            for t in range(3):
                send_p[p * 2 + c, t] = tiles[t].astype(BF16)

        @pl.when(p < WINDOW)
        def _():
            for side in range(2):
                p_copy(side, p).start()

    @pl.when(holds)
    def _():
        pltpu.make_async_copy(near_target, near_target, target_sem.at[1]).wait()
        group = lax.broadcasted_iota(jnp.int32, (8 * PEERS, LANES), 0)
        for k in range(4):
            named = near_target[16 * k]
            for t in range(1, 16):
                named = named + near_target[16 * k + t]
            for ch in range(CHUNKS):
                onehot[ch, :, k * LANES : (k + 1) * LANES] = jnp.where(
                    group == named[ch : ch + 1, :], 1.0, 0.0
                ).astype(BF16)

    def ways(p):
        odd = lax.rem(p, 2)
        ahead = lax.rem(me + 3 + 2 * odd, 4)
        behind = lax.rem(me + 1 + 2 * odd, 4)
        return ahead, behind

    def far_copy(p):
        return remote(
            send_far.at[p], near_far.at[p], c_send.at[0, p], c_recv.at[0, p], ways(p)[0]
        )

    def next_copy(p):
        return remote(
            send_next.at[p], near_next.at[p], c_send.at[1, p], c_recv.at[1, p], ways(p)[0]
        )

    def back_copy(p):
        return remote(
            send_back.at[p], near_back.at[p], c_send.at[2, p], c_recv.at[2, p], ways(p)[1]
        )

    def plane_copy(ch, r, target):
        return along_row(
            send_plane.at[ch, r], near_plane.at[ch, tile], plane_send.at[ch], plane_recv.at[ch],
            target,
        )

    def forward(p):
        far_copy(p).wait_recv()
        for t in range(3):
            send_next[p, t] = (hold_next[p, t] + near_far[p, t].astype(F32)).astype(BF16)
        next_copy(p).start()

    def finish(p):
        next_copy(p).wait_recv()
        back_copy(p).wait_recv()
        tiles = [
            hold_own[p, t] + near_next[p, t].astype(F32) + near_back[p, t].astype(F32)
            for t in range(3)
        ]
        tiles.append(unpack_last(*tiles))
        for e in range(4):
            at = (e % 2) * 8 + lax.rem(p, 4) * 2 + e // 2
            staging[pl.ds(at, PLANES, stride=16), :] = tiles[e]

        @pl.when(lax.rem(p, 4) == 3)
        def _():
            ch = p // 4

            @pl.loop(0, PLANES)
            def _(d):
                r = lax.rem(z * 6 + d, PLANES)
                target = plane_device(r)
                rows = pl.ds(pl.multiple_of(r * 16, 16), 16)
                send_plane[ch, r] = staging[rows, :].astype(BF16)

                @pl.when(target != tile)
                def _():
                    plane_copy(ch, r, target).start()

                @pl.when(target == tile)
                def _():
                    pltpu.make_async_copy(
                        send_plane.at[ch, r], near_plane.at[ch, tile], plane_recv.at[ch]
                    ).start()

    @pl.loop(0, PAIRS)
    def _(p):
        for side in range(2):
            p_copy(side, p).wait_recv()
        for c in range(2):
            for side in range(2):
                tiles = [near_p[side, p * 2 + c, t] for t in range(3)]
                last = unpack_last(*[tile.astype(F32) for tile in tiles]).astype(BF16)
                tiles.append(last)
                for e in range(4):
                    lanes = slice((e % 2) * LANES, (e % 2 + 1) * LANES)
                    rim[c * 7 + 4 * side + e // 2, :, lanes] = tiles[e]
            for k in range(2):
                rim[c * 7 + 2 + k] = own_p[p * 4 + c * 2 + k]
            total = None
            for k in range(2):
                row = p * 4 + c * 2 + k
                stiff = apply(row, c * 7, 2 + k).astype(BF16)
                term = lax.dot_general(
                    rim[c * 7 + 2 + k], stiff, (((0,), (0,)), ((), ())),
                    preferred_element_type=F32,
                )
                total = term if total is None else total + term
            part[c] = total

        def share(col):
            start = pl.multiple_of((col // 2) * LANES + lax.rem(col, 2) * 48, 16)
            rows = pl.ds(start, 48)
            return pack4(
                part[0, rows, 0:LANES],
                part[0, rows, LANES : 2 * LANES],
                part[1, rows, 0:LANES],
                part[1, rows, LANES : 2 * LANES],
            )

        ahead, behind = ways(p)
        tiles = share(lax.rem(me + 2, 4))
        for t in range(3):
            send_far[p, t] = tiles[t].astype(BF16)
        far_copy(p).start()
        tiles = share(behind)
        for t in range(3):
            send_back[p, t] = tiles[t].astype(BF16)
        back_copy(p).start()

        @pl.when(p + WINDOW < PAIRS)
        def _():
            for side in range(2):
                p_copy(side, p + WINDOW).start()

        tiles = share(ahead)
        for t in range(3):
            hold_next[p, t] = tiles[t]
        tiles = share(me)
        for t in range(3):
            hold_own[p, t] = tiles[t]

        @pl.when(p >= LAG)
        def _():
            forward(p - LAG)

        @pl.when(p >= 2 * LAG)
        def _():
            finish(p - 2 * LAG)

    @pl.loop(PAIRS - LAG, PAIRS)
    def _(p):
        forward(p)

    @pl.loop(PAIRS - 2 * LAG, PAIRS)
    def _(p):
        finish(p)

    def group_copy(target):
        return along_row(
            send_group.at[target], near_group.at[plane], group_sem.at[0], group_sem.at[1], target
        )

    @pl.when(holds)
    def _():
        for ch in range(CHUNKS):
            here = near_plane.at[ch]
            pltpu.make_async_copy(here, here, plane_recv.at[ch]).wait()
            rows = near_plane[ch].astype(F32)
            both = [rows[:, c * 8 : c * 8 + 8, :].reshape(8 * PEERS, LANES) for c in range(2)]
            block = jnp.concatenate(both, axis=1).astype(BF16)
            term = dot(onehot[ch], block)
            total_sum[...] = term if ch == 0 else total_sum[...] + term
        both = [
            total_sum[:, c * LANES : (c + 1) * LANES].reshape(PEERS, 8, LANES) for c in range(2)
        ]
        send_group[...] = jnp.concatenate(both, axis=1).astype(BF16)

        @pl.loop(0, PEERS)
        def _(d):
            target = lax.rem(tile + d, PEERS)

            @pl.when(target != tile)
            def _():
                group_copy(target).start()

            @pl.when(target == tile)
            def _():
                pltpu.make_async_copy(
                    send_group.at[tile], near_group.at[plane], group_sem.at[1]
                ).start()

    pltpu.make_async_copy(near_group, near_group, group_sem.at[1]).wait()
    final[...] = near_group[...].astype(F32).reshape(PLANES * 16, LANES)
    for g in range(8):
        first = final[pl.ds(g, PLANES, stride=16), :]
        second = pltpu.roll(final[pl.ds(8 + g, PLANES, stride=16), :], 96, 1)
        high = lax.broadcasted_iota(jnp.int32, first.shape, 1) >= B
        out_ref[g, :, 0:LANES] = jnp.where(high, second, first)
        out_ref[g, :, LANES : 2 * B] = second[:, 0 : 2 * B - LANES]

    for side in range(2):
        label_copy(side).wait_send()

    @pl.loop(0, PAIRS)
    def _(p):
        for side in range(2):
            t_copy(side, p).wait_send()
            p_copy(side, p).wait_send()
        far_copy(p).wait_send()
        next_copy(p).wait_send()
        back_copy(p).wait_send()

    @pl.loop(0, PLANES)
    def _(r):
        target = plane_device(r)

        @pl.when(target != tile)
        def _():
            target_copy(target).wait_send()
            for ch in range(CHUNKS):
                plane_copy(ch, r, target).wait_send()

    @pl.when(holds)
    def _():
        @pl.loop(1, PEERS)
        def _(d):
            group_copy(lax.rem(tile + d, PEERS)).wait_send()


def galerkin(*operands):
    dma = pltpu.SemaphoreType.DMA
    hbm = pl.BlockSpec(memory_space=pl.ANY)
    scalars = pl.BlockSpec(memory_space=pltpu.SMEM)
    share = (PAIRS, 3, 48, LANES)
    return pl.pallas_call(
        galerkin_kernel,
        out_shape=jax.ShapeDtypeStruct((8, PLANES, 2 * B), F32),
        in_specs=[scalars] * 5 + [hbm] * 4,
        out_specs=pl.BlockSpec(memory_space=pltpu.VMEM),
        scratch_shapes=[
            pltpu.VMEM((ROWS, 4, B, B), BF16),
            pltpu.VMEM((ROWS, B, B), BF16),
            pltpu.VMEM((ROWS, B, B), BF16),
            pltpu.VMEM((ROWS, B, B), BF16),
            pltpu.VMEM((ROWS, B, LANES), BF16),
            pltpu.VMEM((ROWS, LANES), F32),
            pltpu.VMEM((2, ROWS, LANES), F32),
            pltpu.VMEM((PAIRS, 3, B, LANES), BF16),
            pltpu.VMEM((2, PAIRS, 3, B, LANES), BF16),
            pltpu.VMEM((ROWS, B, 2 * LANES), BF16),
            pltpu.VMEM((2 * PAIRS, 3, B, LANES), BF16),
            pltpu.VMEM((2, 2 * PAIRS, 3, B, LANES), BF16),
            pltpu.VMEM((14, B, 2 * LANES), BF16),
            pltpu.VMEM((2, 2 * LANES, 2 * LANES), F32),
            pltpu.VMEM(share, BF16),
            pltpu.VMEM(share, BF16),
            pltpu.VMEM(share, BF16),
            pltpu.VMEM(share, BF16),
            pltpu.VMEM(share, BF16),
            pltpu.VMEM(share, BF16),
            pltpu.VMEM(share, F32),
            pltpu.VMEM(share, F32),
            pltpu.VMEM((PLANES * 16, LANES), F32),
            pltpu.VMEM((8, LANES), jnp.int32),
            pltpu.VMEM((PEERS, 8, LANES), jnp.int32),
            pltpu.VMEM((CHUNKS, 8 * PEERS, 4 * LANES), BF16),
            pltpu.VMEM((CHUNKS, PLANES, 16, LANES), BF16),
            pltpu.VMEM((CHUNKS, PEERS, 16, LANES), BF16),
            pltpu.VMEM((8 * PEERS, 2 * LANES), F32),
            pltpu.VMEM((PEERS, 16, LANES), BF16),
            pltpu.VMEM((PLANES, 16, LANES), BF16),
            pltpu.VMEM((PLANES * 16, LANES), F32),
            dma((3, PAIRS)),
            dma,
            dma((2,)),
            dma((2,)),
            dma((2, PAIRS)),
            dma((2, PAIRS)),
            dma((2, PAIRS)),
            dma((2, PAIRS)),
            dma((3, PAIRS)),
            dma((3, PAIRS)),
            dma((2,)),
            dma((CHUNKS,)),
            dma((CHUNKS,)),
            dma((2,)),
        ],
        compiler_params=pltpu.CompilerParams(
            collective_id=0, has_side_effects=True, vmem_limit_bytes=52 * 1024 * 1024
        ),
    )(*operands)


def on_device(
    off_blocks,
    neighbour,
    active,
    diag_blocks,
    diag_inverse,
    tentative,
    aggregate,
    owner_row,
    owner_group,
):
    return galerkin(
        neighbour.T,
        active.T,
        aggregate,
        owner_row[:, 0],
        owner_group,
        off_blocks,
        diag_blocks,
        diag_inverse,
        tentative,
    )


def solution(mesh):
    return jax.shard_map(
        on_device,
        mesh=mesh,
        in_specs=(
            P(("row", "col"), None, None, None),
            P(("row", "col"), None),
            P(("row", "col"), None),
            P(("row", "col"), None, None),
            P(("row", "col"), None, None),
            P(("row", "col"), None, None),
            P(("row", "col")),
            P("row", None),
            P("row"),
        ),
        out_specs=P("row", "col", None),
        check_vma=False,
    )
```

```python
import jax
import jax.numpy as jnp
from jax import lax
from jax.experimental import pallas as pl
from jax.experimental.pallas import tpu as pltpu
from jax.sharding import PartitionSpec as P

MESH = pl.DeviceIdType.MESH
F32 = jnp.float32
BF16 = jnp.bfloat16
B = 96
LANES = 128
OMEGA = 0.6
ROWS = 64
PAIRS = 16
PEERS = 64
PLANES = 48
CHUNKS = 4
WINDOW = 3
LAG = 3
EARLY = 4
BITS = 6


def pack4(b0, b1, b2, b3):
    high = lax.broadcasted_iota(jnp.int32, b0.shape, 1) >= B
    return (
        jnp.where(high, pltpu.roll(b3, 96, 1), b0),
        jnp.where(high, pltpu.roll(b3, 64, 1), b1),
        jnp.where(high, pltpu.roll(b3, 32, 1), b2),
    )


def unpack_last(t0, t1, t2):
    lane = lax.broadcasted_iota(jnp.int32, t0.shape, 1)
    return jnp.where(
        lane < 32,
        pltpu.roll(t0, 32, 1),
        jnp.where(lane < 64, pltpu.roll(t1, 64, 1), pltpu.roll(t2, 96, 1)),
    )


def dot(a, b):
    return lax.dot_general(a, b, (((1,), (0,)), ((), ())), preferred_element_type=F32)


def plane_device(r):
    z = r // 6
    return z * 8 + lax.rem(lax.rem(r, 6) + 2 * z + 2, 8)


def galerkin_kernel(
    near_hbm,
    active_hbm,
    label_hbm,
    owner_hbm,
    group_hbm,
    off_hbm,
    diag_hbm,
    inv_hbm,
    tent_hbm,
    out_ref,
    near_smem,
    active_smem,
    label_smem,
    owner_smem,
    group_smem,
    off,
    diag,
    inv,
    tent,
    wide,
    send_label,
    near_label,
    send_t,
    near_t,
    own_p,
    send_p,
    near_p,
    rim,
    part,
    send_far,
    send_next,
    send_back,
    near_far,
    near_next,
    near_back,
    hold_next,
    hold_own,
    staging,
    send_target,
    near_target,
    onehot,
    send_plane,
    near_plane,
    total_sum,
    send_group,
    near_group,
    final,
    load_sem,
    tent_sem,
    small_sem,
    round_sem,
    label_send,
    label_recv,
    t_send,
    t_recv,
    p_send,
    p_recv,
    c_send,
    c_recv,
    target_sem,
    plane_send,
    plane_recv,
    group_sem,
):
    me = lax.axis_index("col")
    right, left = lax.rem(me + 1, 4), lax.rem(me + 3, 4)
    tile = lax.axis_index("row")
    z = tile // 8
    place = lax.rem(lax.rem(tile, 8) + 32 - 2 * z - 2, 8)
    holds = place < 6
    plane = z * 6 + place

    def loads(p):
        rows = pl.ds(p * 4, 4)
        return [
            pltpu.make_async_copy(off_hbm.at[rows], off.at[rows], load_sem.at[0, p]),
            pltpu.make_async_copy(diag_hbm.at[rows], diag.at[rows], load_sem.at[1, p]),
            pltpu.make_async_copy(inv_hbm.at[rows], inv.at[rows], load_sem.at[2, p]),
        ]

    def remote(src, dst, send_sem, recv_sem, col):
        return pltpu.make_async_remote_copy(
            src_ref=src,
            dst_ref=dst,
            send_sem=send_sem,
            recv_sem=recv_sem,
            device_id={"col": col},
            device_id_type=MESH,
        )

    def along_row(src, dst, send_sem, recv_sem, target):
        return pltpu.make_async_remote_copy(
            src_ref=src,
            dst_ref=dst,
            send_sem=send_sem,
            recv_sem=recv_sem,
            device_id={"row": target},
            device_id_type=MESH,
        )

    def tent_load(p):
        rows = pl.ds(p * 4, 4)
        return pltpu.make_async_copy(tent_hbm.at[rows], tent.at[rows], tent_sem.at[p])

    small = [
        pltpu.make_async_copy(src, dst, small_sem.at[i])
        for i, (src, dst) in enumerate(
            [
                (label_hbm, label_smem),
                (near_hbm, near_smem),
                (active_hbm, active_smem),
                (owner_hbm, owner_smem),
                (group_hbm, group_smem),
            ]
        )
    ]

    def partner(b):
        size = 1 << b
        return tile + size * (1 - 2 * lax.rem(tile // size, 2))

    barrier = pltpu.get_barrier_semaphore()
    for peer in (left, right):
        pl.semaphore_signal(barrier, inc=1, device_id={"col": peer}, device_id_type=MESH)
    for b in range(BITS):
        pl.semaphore_signal(barrier, inc=1, device_id={"row": partner(b)}, device_id_type=MESH)

    for copy in small:
        copy.start()

    @pl.loop(0, PAIRS)
    def _(p):
        tent_load(p).start()

    small[0].wait()

    @pl.loop(0, ROWS)
    def _(f):
        send_label[pl.ds(f, 1), :] = jnp.full((1, LANES), label_smem[f], jnp.int32).astype(F32)

    def pack_tent(p):
        tent_load(p).wait()
        for e in range(4):
            wide[p * 4 + e, :, 0:B] = tent[p * 4 + e]
        tiles = pack4(*[wide[p * 4 + e].astype(F32) for e in range(4)])
        for t in range(3):
            send_t[p, t] = tiles[t].astype(BF16)

    @pl.loop(0, EARLY)
    def _(p):
        pack_tent(p)

    pl.semaphore_wait(barrier, 2 + BITS)

    def label_copy(side):
        return remote(
            send_label, near_label.at[side], label_send.at[side], label_recv.at[side],
            right if side == 0 else left,
        )

    def t_copy(side, p):
        return remote(
            send_t.at[p], near_t.at[side, p], t_send.at[side, p], t_recv.at[side, p],
            right if side == 0 else left,
        )

    def p_copy(side, p):
        rows = pl.ds(p * 2, 2)
        return remote(
            send_p.at[rows], near_p.at[side, rows], p_send.at[side, p], p_recv.at[side, p],
            right if side == 0 else left,
        )

    def target_copy(target):
        return along_row(
            send_target, near_target.at[tile], target_sem.at[0], target_sem.at[1], target
        )

    for side in range(2):
        label_copy(side).start()

    @pl.loop(0, PAIRS)
    def _(p):
        @pl.when(p >= EARLY)
        def _():
            pack_tent(p)

        for side in range(2):
            t_copy(side, p).start()

    @pl.loop(0, PAIRS)
    def _(p):
        for copy in loads(p):
            copy.start()

    rim[6] = jnp.zeros_like(rim[6])
    rim[13] = jnp.zeros_like(rim[13])

    for b in range(BITS):
        pl.semaphore_signal(
            round_sem.at[b], inc=1, device_id={"row": partner(b)}, device_id_type=MESH
        )
        pl.semaphore_wait(round_sem.at[b], 1)

    for copy in small[1:]:
        copy.wait()
    sub = lax.broadcasted_iota(jnp.int32, (8, LANES), 0)
    lane = lax.broadcasted_iota(jnp.int32, (8, LANES), 1)
    mine = jnp.zeros((8, LANES), jnp.int32)
    for q in range(32):
        here = (sub == q // 8) & (lane == lax.rem(tile, 16) * 8 + q % 8)
        mine = jnp.where(here, owner_smem[q] * 8 + group_smem[q], mine)
    send_target[...] = mine

    @pl.loop(0, PLANES)
    def _(d):
        target = plane_device(lax.rem(tile + d, PLANES))

        @pl.when(target != tile)
        def _():
            target_copy(target).start()

    @pl.when(holds)
    def _():
        pltpu.make_async_copy(send_target, near_target.at[tile], target_sem.at[1]).start()

    for side in range(2):
        label_copy(side).wait_recv()

    def apply(row, near_base, own):
        total = dot(diag[row], rim[near_base + own])
        for s in range(4):
            on = active_smem[s, row]
            slot = near_smem[s, row] * on + 6 * (1 - on)
            total = total + dot(off[row, s], rim[near_base + slot])
        return total

    @pl.loop(0, PAIRS)
    def _(p):
        for side in range(2):
            t_copy(side, p).wait_recv()
        for copy in loads(p):
            copy.wait()

        def spread(e, position, block, label):
            zero = jnp.zeros_like(block)
            at = (e // 2) * 7 + position + e % 2
            rim[at, :, 0:LANES] = jnp.where(label == 0.0, block, zero).astype(BF16)
            rim[at, :, LANES : 2 * LANES] = jnp.where(label == 1.0, block, zero).astype(BF16)

        for side in range(2):
            tiles = [near_t[side, p, t].astype(F32) for t in range(3)]
            tiles.append(unpack_last(*tiles))
            for e in range(4):
                spread(e, 4 * side, tiles[e], near_label[side, pl.ds(p * 4 + e, 1), :])
        for e in range(4):
            spread(e, 2, wide[p * 4 + e].astype(F32), send_label[pl.ds(p * 4 + e, 1), :])

        for c in range(2):
            blocks = []
            for k in range(2):
                row = p * 4 + c * 2 + k
                smooth = apply(row, c * 7, 2 + k).astype(BF16)
                prolong = rim[c * 7 + 2 + k].astype(F32) - OMEGA * dot(inv[row], smooth)
                rounded = prolong.astype(BF16)
                own_p[row] = rounded
                back = rounded.astype(F32)
                blocks += [back[:, 0:LANES], back[:, LANES : 2 * LANES]]
            tiles = pack4(*blocks)
            for t in range(3):
                send_p[p * 2 + c, t] = tiles[t].astype(BF16)

        @pl.when(p < WINDOW)
        def _():
            for side in range(2):
                p_copy(side, p).start()

    @pl.when(holds)
    def _():
        pltpu.make_async_copy(near_target, near_target, target_sem.at[1]).wait()
        group = lax.broadcasted_iota(jnp.int32, (8 * PEERS, LANES), 0)
        for k in range(4):
            named = near_target[16 * k]
            for t in range(1, 16):
                named = named + near_target[16 * k + t]
            for ch in range(CHUNKS):
                onehot[ch, :, k * LANES : (k + 1) * LANES] = jnp.where(
                    group == named[ch : ch + 1, :], 1.0, 0.0
                ).astype(BF16)

    def ways(p):
        odd = lax.rem(p, 2)
        ahead = lax.rem(me + 3 + 2 * odd, 4)
        behind = lax.rem(me + 1 + 2 * odd, 4)
        return ahead, behind

    def far_copy(p):
        return remote(
            send_far.at[p], near_far.at[p], c_send.at[0, p], c_recv.at[0, p], ways(p)[0]
        )

    def next_copy(p):
        return remote(
            send_next.at[p], near_next.at[p], c_send.at[1, p], c_recv.at[1, p], ways(p)[0]
        )

    def back_copy(p):
        return remote(
            send_back.at[p], near_back.at[p], c_send.at[2, p], c_recv.at[2, p], ways(p)[1]
        )

    def plane_copy(ch, r, target):
        return along_row(
            send_plane.at[ch, r], near_plane.at[ch, tile], plane_send.at[ch], plane_recv.at[ch],
            target,
        )

    def forward(p):
        far_copy(p).wait_recv()
        for t in range(3):
            send_next[p, t] = (hold_next[p, t] + near_far[p, t].astype(F32)).astype(BF16)
        next_copy(p).start()

    def finish(p):
        next_copy(p).wait_recv()
        back_copy(p).wait_recv()
        tiles = [
            hold_own[p, t] + near_next[p, t].astype(F32) + near_back[p, t].astype(F32)
            for t in range(3)
        ]
        tiles.append(unpack_last(*tiles))
        for e in range(4):
            at = (e % 2) * 8 + lax.rem(p, 4) * 2 + e // 2
            staging[pl.ds(at, PLANES, stride=16), :] = tiles[e]

        @pl.when(lax.rem(p, 4) == 3)
        def _():
            ch = p // 4

            @pl.loop(0, PLANES)
            def _(d):
                r = lax.rem(tile + d, PLANES)
                target = plane_device(r)
                rows = pl.ds(pl.multiple_of(r * 16, 16), 16)
                send_plane[ch, r] = staging[rows, :].astype(BF16)

                @pl.when(target != tile)
                def _():
                    plane_copy(ch, r, target).start()

                @pl.when(target == tile)
                def _():
                    pltpu.make_async_copy(
                        send_plane.at[ch, r], near_plane.at[ch, tile], plane_recv.at[ch]
                    ).start()

    @pl.loop(0, PAIRS)
    def _(p):
        for side in range(2):
            p_copy(side, p).wait_recv()
        for c in range(2):
            for side in range(2):
                tiles = [near_p[side, p * 2 + c, t] for t in range(3)]
                last = unpack_last(*[tile.astype(F32) for tile in tiles]).astype(BF16)
                tiles.append(last)
                for e in range(4):
                    lanes = slice((e % 2) * LANES, (e % 2 + 1) * LANES)
                    rim[c * 7 + 4 * side + e // 2, :, lanes] = tiles[e]
            for k in range(2):
                rim[c * 7 + 2 + k] = own_p[p * 4 + c * 2 + k]
            total = None
            for k in range(2):
                row = p * 4 + c * 2 + k
                stiff = apply(row, c * 7, 2 + k).astype(BF16)
                term = lax.dot_general(
                    rim[c * 7 + 2 + k], stiff, (((0,), (0,)), ((), ())),
                    preferred_element_type=F32,
                )
                total = term if total is None else total + term
            part[c] = total

        def share(col):
            start = pl.multiple_of((col // 2) * LANES + lax.rem(col, 2) * 48, 16)
            rows = pl.ds(start, 48)
            return pack4(
                part[0, rows, 0:LANES],
                part[0, rows, LANES : 2 * LANES],
                part[1, rows, 0:LANES],
                part[1, rows, LANES : 2 * LANES],
            )

        ahead, behind = ways(p)
        tiles = share(lax.rem(me + 2, 4))
        for t in range(3):
            send_far[p, t] = tiles[t].astype(BF16)
        far_copy(p).start()
        tiles = share(behind)
        for t in range(3):
            send_back[p, t] = tiles[t].astype(BF16)
        back_copy(p).start()

        @pl.when(p + WINDOW < PAIRS)
        def _():
            for side in range(2):
                p_copy(side, p + WINDOW).start()

        tiles = share(ahead)
        for t in range(3):
            hold_next[p, t] = tiles[t]
        tiles = share(me)
        for t in range(3):
            hold_own[p, t] = tiles[t]

        @pl.when(p >= LAG)
        def _():
            forward(p - LAG)

        @pl.when(p >= 2 * LAG)
        def _():
            finish(p - 2 * LAG)

    @pl.loop(PAIRS - LAG, PAIRS)
    def _(p):
        forward(p)

    @pl.loop(PAIRS - 2 * LAG, PAIRS)
    def _(p):
        finish(p)

    def group_copy(target):
        return along_row(
            send_group.at[target], near_group.at[plane], group_sem.at[0], group_sem.at[1], target
        )

    @pl.when(holds)
    def _():
        for ch in range(CHUNKS):
            here = near_plane.at[ch]
            pltpu.make_async_copy(here, here, plane_recv.at[ch]).wait()
            rows = near_plane[ch].astype(F32)
            both = [rows[:, c * 8 : c * 8 + 8, :].reshape(8 * PEERS, LANES) for c in range(2)]
            block = jnp.concatenate(both, axis=1).astype(BF16)
            term = dot(onehot[ch], block)
            total_sum[...] = term if ch == 0 else total_sum[...] + term
        both = [
            total_sum[:, c * LANES : (c + 1) * LANES].reshape(PEERS, 8, LANES) for c in range(2)
        ]
        send_group[...] = jnp.concatenate(both, axis=1).astype(BF16)

        @pl.loop(0, PEERS)
        def _(d):
            target = lax.rem(tile + d, PEERS)

            @pl.when(target != tile)
            def _():
                group_copy(target).start()

            @pl.when(target == tile)
            def _():
                pltpu.make_async_copy(
                    send_group.at[tile], near_group.at[plane], group_sem.at[1]
                ).start()

    for side in range(2):
        label_copy(side).wait_send()

    @pl.loop(0, PAIRS)
    def _(p):
        for side in range(2):
            t_copy(side, p).wait_send()
            p_copy(side, p).wait_send()
        far_copy(p).wait_send()
        next_copy(p).wait_send()
        back_copy(p).wait_send()

    @pl.loop(0, PLANES)
    def _(r):
        target = plane_device(r)

        @pl.when(target != tile)
        def _():
            target_copy(target).wait_send()
            for ch in range(CHUNKS):
                plane_copy(ch, r, target).wait_send()

    pltpu.make_async_copy(near_group, near_group, group_sem.at[1]).wait()
    final[...] = near_group[...].astype(F32).reshape(PLANES * 16, LANES)
    for g in range(8):
        first = final[pl.ds(g, PLANES, stride=16), :]
        second = pltpu.roll(final[pl.ds(8 + g, PLANES, stride=16), :], 96, 1)
        high = lax.broadcasted_iota(jnp.int32, first.shape, 1) >= B
        out_ref[g, :, 0:LANES] = jnp.where(high, second, first)
        out_ref[g, :, LANES : 2 * B] = second[:, 0 : 2 * B - LANES]

    @pl.when(holds)
    def _():
        @pl.loop(1, PEERS)
        def _(d):
            group_copy(lax.rem(tile + d, PEERS)).wait_send()


def galerkin(*operands):
    dma = pltpu.SemaphoreType.DMA
    hbm = pl.BlockSpec(memory_space=pltpu.HBM)
    share = (PAIRS, 3, 48, LANES)
    return pl.pallas_call(
        galerkin_kernel,
        out_shape=jax.ShapeDtypeStruct((8, PLANES, 2 * B), F32),
        in_specs=[hbm] * 9,
        out_specs=pl.BlockSpec(memory_space=pltpu.VMEM),
        scratch_shapes=[
            pltpu.SMEM((4, ROWS), jnp.int32),
            pltpu.SMEM((4, ROWS), jnp.int32),
            pltpu.SMEM((ROWS,), jnp.int32),
            pltpu.SMEM((32,), jnp.int32),
            pltpu.SMEM((32,), jnp.int32),
            pltpu.VMEM((ROWS, 4, B, B), BF16),
            pltpu.VMEM((ROWS, B, B), BF16),
            pltpu.VMEM((ROWS, B, B), BF16),
            pltpu.VMEM((ROWS, B, B), BF16),
            pltpu.VMEM((ROWS, B, LANES), BF16),
            pltpu.VMEM((ROWS, LANES), F32),
            pltpu.VMEM((2, ROWS, LANES), F32),
            pltpu.VMEM((PAIRS, 3, B, LANES), BF16),
            pltpu.VMEM((2, PAIRS, 3, B, LANES), BF16),
            pltpu.VMEM((ROWS, B, 2 * LANES), BF16),
            pltpu.VMEM((2 * PAIRS, 3, B, LANES), BF16),
            pltpu.VMEM((2, 2 * PAIRS, 3, B, LANES), BF16),
            pltpu.VMEM((14, B, 2 * LANES), BF16),
            pltpu.VMEM((2, 2 * LANES, 2 * LANES), F32),
            pltpu.VMEM(share, BF16),
            pltpu.VMEM(share, BF16),
            pltpu.VMEM(share, BF16),
            pltpu.VMEM(share, BF16),
            pltpu.VMEM(share, BF16),
            pltpu.VMEM(share, BF16),
            pltpu.VMEM(share, F32),
            pltpu.VMEM(share, F32),
            pltpu.VMEM((PLANES * 16, LANES), F32),
            pltpu.VMEM((8, LANES), jnp.int32),
            pltpu.VMEM((PEERS, 8, LANES), jnp.int32),
            pltpu.VMEM((CHUNKS, 8 * PEERS, 4 * LANES), BF16),
            pltpu.VMEM((CHUNKS, PLANES, 16, LANES), BF16),
            pltpu.VMEM((CHUNKS, PEERS, 16, LANES), BF16),
            pltpu.VMEM((8 * PEERS, 2 * LANES), F32),
            pltpu.VMEM((PEERS, 16, LANES), BF16),
            pltpu.VMEM((PLANES, 16, LANES), BF16),
            pltpu.VMEM((PLANES * 16, LANES), F32),
            dma((3, PAIRS)),
            dma((PAIRS,)),
            dma((5,)),
            pltpu.SemaphoreType.REGULAR((BITS,)),
            dma((2,)),
            dma((2,)),
            dma((2, PAIRS)),
            dma((2, PAIRS)),
            dma((2, PAIRS)),
            dma((2, PAIRS)),
            dma((3, PAIRS)),
            dma((3, PAIRS)),
            dma((2,)),
            dma((CHUNKS,)),
            dma((CHUNKS,)),
            dma((2,)),
        ],
        compiler_params=pltpu.CompilerParams(
            collective_id=0, has_side_effects=True, vmem_limit_bytes=62 * 1024 * 1024
        ),
    )(*operands)


def on_device(
    off_blocks,
    neighbour,
    active,
    diag_blocks,
    diag_inverse,
    tentative,
    aggregate,
    owner_row,
    owner_group,
):
    return galerkin(
        neighbour.T,
        active.T,
        aggregate,
        owner_row[:, 0],
        owner_group,
        off_blocks,
        diag_blocks,
        diag_inverse,
        tentative,
    )


def solution(mesh):
    return jax.shard_map(
        on_device,
        mesh=mesh,
        in_specs=(
            P(("row", "col"), None, None, None),
            P(("row", "col"), None),
            P(("row", "col"), None),
            P(("row", "col"), None, None),
            P(("row", "col"), None, None),
            P(("row", "col"), None, None),
            P(("row", "col")),
            P("row", None),
            P("row"),
        ),
        out_specs=P("row", "col", None),
        check_vma=False,
    )
```

```python
import jax
import jax.numpy as jnp
from jax import lax
from jax.experimental import pallas as pl
from jax.experimental.pallas import tpu as pltpu
from jax.sharding import PartitionSpec as P

MESH = pl.DeviceIdType.MESH
F32 = jnp.float32
BF16 = jnp.bfloat16
B = 96
LANES = 128
OMEGA = 0.6
ROWS = 64
PAIRS = 16
PEERS = 64
PLANES = 48
CHUNKS = 4
WINDOW = 3
LAG = 3
DIRECT = 14
EARLY = 1
BITS = 6


def pack4(b0, b1, b2, b3):
    high = lax.broadcasted_iota(jnp.int32, b0.shape, 1) >= B
    return (
        jnp.where(high, pltpu.roll(b3, 96, 1), b0),
        jnp.where(high, pltpu.roll(b3, 64, 1), b1),
        jnp.where(high, pltpu.roll(b3, 32, 1), b2),
    )


def unpack_last(t0, t1, t2):
    lane = lax.broadcasted_iota(jnp.int32, t0.shape, 1)
    return jnp.where(
        lane < 32,
        pltpu.roll(t0, 32, 1),
        jnp.where(lane < 64, pltpu.roll(t1, 64, 1), pltpu.roll(t2, 96, 1)),
    )


def dot(a, b):
    return lax.dot_general(a, b, (((1,), (0,)), ((), ())), preferred_element_type=F32)


def plane_device(r):
    z = r // 6
    return z * 8 + lax.rem(lax.rem(r, 6) + 2 * z + 2, 8)


def galerkin_kernel(
    near_hbm,
    active_hbm,
    label_hbm,
    owner_hbm,
    group_hbm,
    off_hbm,
    diag_hbm,
    inv_hbm,
    tent_hbm,
    out_ref,
    near_smem,
    active_smem,
    label_smem,
    owner_smem,
    group_smem,
    off,
    diag,
    inv,
    tent,
    wide,
    send_label,
    near_label,
    send_t,
    near_t,
    own_p,
    send_p,
    near_p,
    rim,
    part,
    send_far,
    send_next,
    send_back,
    near_far,
    near_next,
    near_back,
    hold_next,
    hold_own,
    staging,
    send_target,
    near_target,
    onehot,
    send_plane,
    near_plane,
    total_sum,
    send_group,
    near_group,
    final,
    load_sem,
    tent_sem,
    small_sem,
    round_sem,
    label_send,
    label_recv,
    t_send,
    t_recv,
    p_send,
    p_recv,
    c_send,
    c_recv,
    target_sem,
    plane_send,
    plane_recv,
    group_sem,
):
    me = lax.axis_index("col")
    right, left, opposite = [lax.rem(me + d, 4) for d in (1, 3, 2)]
    tile = lax.axis_index("row")
    z = tile // 8
    place = lax.rem(lax.rem(tile, 8) + 32 - 2 * z - 2, 8)
    holds = place < 6
    plane = z * 6 + place

    def loads(p):
        rows = pl.ds(p * 4, 4)
        return [
            pltpu.make_async_copy(off_hbm.at[rows], off.at[rows], load_sem.at[0, p]),
            pltpu.make_async_copy(diag_hbm.at[rows], diag.at[rows], load_sem.at[1, p]),
            pltpu.make_async_copy(inv_hbm.at[rows], inv.at[rows], load_sem.at[2, p]),
        ]

    def remote(src, dst, send_sem, recv_sem, col):
        return pltpu.make_async_remote_copy(
            src_ref=src,
            dst_ref=dst,
            send_sem=send_sem,
            recv_sem=recv_sem,
            device_id={"col": col},
            device_id_type=MESH,
        )

    def along_row(src, dst, send_sem, recv_sem, target):
        return pltpu.make_async_remote_copy(
            src_ref=src,
            dst_ref=dst,
            send_sem=send_sem,
            recv_sem=recv_sem,
            device_id={"row": target},
            device_id_type=MESH,
        )

    def tent_load(p):
        rows = pl.ds(p * 4, 4)
        return pltpu.make_async_copy(tent_hbm.at[rows], tent.at[rows], tent_sem.at[p])

    small = [
        pltpu.make_async_copy(src, dst, small_sem.at[i])
        for i, (src, dst) in enumerate(
            [
                (label_hbm, label_smem),
                (near_hbm, near_smem),
                (active_hbm, active_smem),
                (owner_hbm, owner_smem),
                (group_hbm, group_smem),
            ]
        )
    ]

    def partner(b):
        size = 1 << b
        return tile + size * (1 - 2 * lax.rem(tile // size, 2))

    barrier = pltpu.get_barrier_semaphore()
    for peer in (left, right, opposite):
        pl.semaphore_signal(barrier, inc=1, device_id={"col": peer}, device_id_type=MESH)
    for b in range(BITS):
        pl.semaphore_signal(barrier, inc=1, device_id={"row": partner(b)}, device_id_type=MESH)

    for copy in small:
        copy.start()

    @pl.loop(0, PAIRS)
    def _(p):
        tent_load(p).start()

    small[0].wait()

    @pl.loop(0, ROWS)
    def _(f):
        send_label[pl.ds(f, 1), :] = jnp.full((1, LANES), label_smem[f], jnp.int32).astype(F32)

    def pack_tent(p):
        tent_load(p).wait()
        for e in range(4):
            wide[p * 4 + e, :, 0:B] = tent[p * 4 + e]
        tiles = pack4(*[wide[p * 4 + e].astype(F32) for e in range(4)])
        for t in range(3):
            send_t[p, t] = tiles[t].astype(BF16)

    @pl.loop(0, EARLY)
    def _(p):
        pack_tent(p)

    pl.semaphore_wait(barrier, 3 + BITS)

    def label_copy(side):
        return remote(
            send_label, near_label.at[side], label_send.at[side], label_recv.at[side],
            right if side == 0 else left,
        )

    def t_copy(side, p):
        return remote(
            send_t.at[p], near_t.at[side, p], t_send.at[side, p], t_recv.at[side, p],
            right if side == 0 else left,
        )

    def p_copy(side, p):
        rows = pl.ds(p * 2, 2)
        return remote(
            send_p.at[rows], near_p.at[side, rows], p_send.at[side, p], p_recv.at[side, p],
            right if side == 0 else left,
        )

    def target_copy(target):
        return along_row(
            send_target, near_target.at[tile], target_sem.at[0], target_sem.at[1], target
        )

    for side in range(2):
        label_copy(side).start()

    @pl.loop(0, PAIRS)
    def _(p):
        @pl.when(p >= EARLY)
        def _():
            pack_tent(p)

        for side in range(2):
            t_copy(side, p).start()

    @pl.loop(0, PAIRS)
    def _(p):
        for copy in loads(p):
            copy.start()

    rim[6] = jnp.zeros_like(rim[6])
    rim[13] = jnp.zeros_like(rim[13])

    for b in range(BITS):
        pl.semaphore_signal(
            round_sem.at[b], inc=1, device_id={"row": partner(b)}, device_id_type=MESH
        )
        pl.semaphore_wait(round_sem.at[b], 1)

    for copy in small[1:]:
        copy.wait()
    sub = lax.broadcasted_iota(jnp.int32, (8, LANES), 0)
    lane = lax.broadcasted_iota(jnp.int32, (8, LANES), 1)
    mine = jnp.zeros((8, LANES), jnp.int32)
    for q in range(32):
        here = (sub == q // 8) & (lane == lax.rem(tile, 16) * 8 + q % 8)
        mine = jnp.where(here, owner_smem[q] * 8 + group_smem[q], mine)
    send_target[...] = mine

    @pl.loop(0, PLANES)
    def _(d):
        target = plane_device(lax.rem(tile + d, PLANES))

        @pl.when(target != tile)
        def _():
            target_copy(target).start()

    @pl.when(holds)
    def _():
        pltpu.make_async_copy(send_target, near_target.at[tile], target_sem.at[1]).start()

    for side in range(2):
        label_copy(side).wait_recv()

    def apply(row, near_base, own):
        total = dot(diag[row], rim[near_base + own])
        for s in range(4):
            on = active_smem[s, row]
            slot = near_smem[s, row] * on + 6 * (1 - on)
            total = total + dot(off[row, s], rim[near_base + slot])
        return total

    @pl.loop(0, PAIRS)
    def _(p):
        for side in range(2):
            t_copy(side, p).wait_recv()
        for copy in loads(p):
            copy.wait()

        def spread(e, position, block, label):
            zero = jnp.zeros_like(block)
            at = (e // 2) * 7 + position + e % 2
            rim[at, :, 0:LANES] = jnp.where(label == 0.0, block, zero).astype(BF16)
            rim[at, :, LANES : 2 * LANES] = jnp.where(label == 1.0, block, zero).astype(BF16)

        for side in range(2):
            tiles = [near_t[side, p, t].astype(F32) for t in range(3)]
            tiles.append(unpack_last(*tiles))
            for e in range(4):
                spread(e, 4 * side, tiles[e], near_label[side, pl.ds(p * 4 + e, 1), :])
        for e in range(4):
            spread(e, 2, wide[p * 4 + e].astype(F32), send_label[pl.ds(p * 4 + e, 1), :])

        for c in range(2):
            blocks = []
            for k in range(2):
                row = p * 4 + c * 2 + k
                smooth = apply(row, c * 7, 2 + k).astype(BF16)
                prolong = rim[c * 7 + 2 + k].astype(F32) - OMEGA * dot(inv[row], smooth)
                rounded = prolong.astype(BF16)
                own_p[row] = rounded
                back = rounded.astype(F32)
                blocks += [back[:, 0:LANES], back[:, LANES : 2 * LANES]]
            tiles = pack4(*blocks)
            for t in range(3):
                send_p[p * 2 + c, t] = tiles[t].astype(BF16)

        @pl.when(p < WINDOW)
        def _():
            for side in range(2):
                p_copy(side, p).start()

    @pl.when(holds)
    def _():
        pltpu.make_async_copy(near_target, near_target, target_sem.at[1]).wait()
        group = lax.broadcasted_iota(jnp.int32, (8 * PEERS, LANES), 0)
        for k in range(4):
            named = near_target[16 * k]
            for t in range(1, 16):
                named = named + near_target[16 * k + t]
            for ch in range(CHUNKS):
                onehot[ch, :, k * LANES : (k + 1) * LANES] = jnp.where(
                    group == named[ch : ch + 1, :], 1.0, 0.0
                ).astype(BF16)

    def ways(p):
        odd = p % 2
        ahead = lax.rem(me + 3 + 2 * odd, 4)
        behind = lax.rem(me + 1 + 2 * odd, 4)
        return ahead, behind

    def far_copy(p, direct=False):
        return remote(
            send_far.at[p], near_far.at[p], c_send.at[0, p], c_recv.at[0, p],
            opposite if direct else ways(p)[0],
        )

    def next_copy(p):
        return remote(
            send_next.at[p], near_next.at[p], c_send.at[1, p], c_recv.at[1, p], ways(p)[0]
        )

    def back_copy(p):
        return remote(
            send_back.at[p], near_back.at[p], c_send.at[2, p], c_recv.at[2, p], ways(p)[1]
        )

    def plane_copy(ch, r, target):
        return along_row(
            send_plane.at[ch, r], near_plane.at[ch, tile], plane_send.at[ch], plane_recv.at[ch],
            target,
        )

    def forward(p):
        far_copy(p).wait_recv()
        for t in range(3):
            send_next[p, t] = (hold_next[p, t] + near_far[p, t].astype(F32)).astype(BF16)
        next_copy(p).start()

    def finish(p, direct=False):
        next_copy(p).wait_recv()
        back_copy(p).wait_recv()
        tiles = [
            hold_own[p, t] + near_next[p, t].astype(F32) + near_back[p, t].astype(F32)
            for t in range(3)
        ]
        if direct:
            far_copy(p, True).wait_recv()
            tiles = [tiles[t] + near_far[p, t].astype(F32) for t in range(3)]
        tiles.append(unpack_last(*tiles))
        for e in range(4):
            at = (e % 2) * 8 + (p % 4) * 2 + e // 2
            staging[pl.ds(at, PLANES, stride=16), :] = tiles[e]

        def send_planes():
            ch = p // 4
            send_plane[ch] = staging[...].reshape(PLANES, 16, LANES).astype(BF16)

            @pl.loop(0, PLANES)
            def _(d):
                r = lax.rem(tile + d, PLANES)
                target = plane_device(r)

                @pl.when(target != tile)
                def _():
                    plane_copy(ch, r, target).start()

                @pl.when(target == tile)
                def _():
                    pltpu.make_async_copy(
                        send_plane.at[ch, r], near_plane.at[ch, tile], plane_recv.at[ch]
                    ).start()

        if isinstance(p, int):
            if p % 4 == 3:
                send_planes()
        else:
            pl.when(lax.rem(p, 4) == 3)(send_planes)

    def products(p, direct=False):
        for side in range(2):
            p_copy(side, p).wait_recv()
        for c in range(2):
            for side in range(2):
                tiles = [near_p[side, p * 2 + c, t] for t in range(3)]
                last = unpack_last(*[tile.astype(F32) for tile in tiles]).astype(BF16)
                tiles.append(last)
                for e in range(4):
                    lanes = slice((e % 2) * LANES, (e % 2 + 1) * LANES)
                    rim[c * 7 + 4 * side + e // 2, :, lanes] = tiles[e]
            for k in range(2):
                rim[c * 7 + 2 + k] = own_p[p * 4 + c * 2 + k]
            total = None
            for k in range(2):
                row = p * 4 + c * 2 + k
                stiff = apply(row, c * 7, 2 + k).astype(BF16)
                term = lax.dot_general(
                    rim[c * 7 + 2 + k], stiff, (((0,), (0,)), ((), ())),
                    preferred_element_type=F32,
                )
                total = term if total is None else total + term
            part[c] = total

        def share(col):
            start = pl.multiple_of((col // 2) * LANES + lax.rem(col, 2) * 48, 16)
            rows = pl.ds(start, 48)
            return pack4(
                part[0, rows, 0:LANES],
                part[0, rows, LANES : 2 * LANES],
                part[1, rows, 0:LANES],
                part[1, rows, LANES : 2 * LANES],
            )

        ahead, behind = ways(p)
        tiles = share(lax.rem(me + 2, 4))
        for t in range(3):
            send_far[p, t] = tiles[t].astype(BF16)
        far_copy(p, direct).start()
        tiles = share(behind)
        for t in range(3):
            send_back[p, t] = tiles[t].astype(BF16)
        back_copy(p).start()

        if not direct:

            @pl.when(p + WINDOW < PAIRS)
            def _():
                for side in range(2):
                    p_copy(side, p + WINDOW).start()

        tiles = share(ahead)
        for t in range(3):
            if direct:
                send_next[p, t] = tiles[t].astype(BF16)
            else:
                hold_next[p, t] = tiles[t]
        if direct:
            next_copy(p).start()
        tiles = share(me)
        for t in range(3):
            hold_own[p, t] = tiles[t]

    @pl.loop(0, DIRECT)
    def _(p):
        products(p)

        @pl.when(p >= LAG)
        def _():
            forward(p - LAG)

        @pl.when(p >= 2 * LAG)
        def _():
            finish(p - 2 * LAG)

    for p in range(DIRECT, PAIRS):
        products(p, True)
        if p - LAG < DIRECT:
            forward(p - LAG)
        finish(p - 2 * LAG)
    for p in range(PAIRS - LAG, DIRECT):
        forward(p)
    for p in range(PAIRS - 2 * LAG, PAIRS):
        finish(p, p >= DIRECT)

    def group_copy(target):
        return along_row(
            send_group.at[target], near_group.at[plane], group_sem.at[0], group_sem.at[1], target
        )

    @pl.when(holds)
    def _():
        for ch in range(CHUNKS):
            here = near_plane.at[ch]
            pltpu.make_async_copy(here, here, plane_recv.at[ch]).wait()
            rows = near_plane[ch].astype(F32)
            both = [rows[:, c * 8 : c * 8 + 8, :].reshape(8 * PEERS, LANES) for c in range(2)]
            block = jnp.concatenate(both, axis=1).astype(BF16)
            term = dot(onehot[ch], block)
            total_sum[...] = term if ch == 0 else total_sum[...] + term
        both = [
            total_sum[:, c * LANES : (c + 1) * LANES].reshape(PEERS, 8, LANES) for c in range(2)
        ]
        send_group[...] = jnp.concatenate(both, axis=1).astype(BF16)

        @pl.loop(0, PEERS)
        def _(d):
            target = lax.rem(tile + d, PEERS)

            @pl.when(target != tile)
            def _():
                group_copy(target).start()

            @pl.when(target == tile)
            def _():
                pltpu.make_async_copy(
                    send_group.at[tile], near_group.at[plane], group_sem.at[1]
                ).start()

    for side in range(2):
        label_copy(side).wait_send()

    @pl.loop(0, PAIRS)
    def _(p):
        for side in range(2):
            t_copy(side, p).wait_send()
            p_copy(side, p).wait_send()
        far_copy(p).wait_send()
        next_copy(p).wait_send()
        back_copy(p).wait_send()

    @pl.loop(0, PLANES)
    def _(r):
        target = plane_device(r)

        @pl.when(target != tile)
        def _():
            target_copy(target).wait_send()
            for ch in range(CHUNKS):
                plane_copy(ch, r, target).wait_send()

    pltpu.make_async_copy(near_group, near_group, group_sem.at[1]).wait()
    final[...] = near_group[...].astype(F32).reshape(PLANES * 16, LANES)
    for g in range(8):
        first = final[pl.ds(g, PLANES, stride=16), :]
        second = pltpu.roll(final[pl.ds(8 + g, PLANES, stride=16), :], 96, 1)
        high = lax.broadcasted_iota(jnp.int32, first.shape, 1) >= B
        out_ref[g, :, 0:LANES] = jnp.where(high, second, first).astype(BF16)
        out_ref[g, :, LANES : 2 * B] = second[:, 0 : 2 * B - LANES].astype(BF16)

    @pl.when(holds)
    def _():
        @pl.loop(1, PEERS)
        def _(d):
            group_copy(lax.rem(tile + d, PEERS)).wait_send()


def galerkin(*operands):
    dma = pltpu.SemaphoreType.DMA
    hbm = pl.BlockSpec(memory_space=pltpu.HBM)
    share = (PAIRS, 3, 48, LANES)
    return pl.pallas_call(
        galerkin_kernel,
        out_shape=jax.ShapeDtypeStruct((8, PLANES, 2 * B), BF16),
        in_specs=[hbm] * 9,
        out_specs=pl.BlockSpec(memory_space=pltpu.VMEM),
        scratch_shapes=[
            pltpu.SMEM((4, ROWS), jnp.int32),
            pltpu.SMEM((4, ROWS), jnp.int32),
            pltpu.SMEM((ROWS,), jnp.int32),
            pltpu.SMEM((32,), jnp.int32),
            pltpu.SMEM((32,), jnp.int32),
            pltpu.VMEM((ROWS, 4, B, B), BF16),
            pltpu.VMEM((ROWS, B, B), BF16),
            pltpu.VMEM((ROWS, B, B), BF16),
            pltpu.VMEM((ROWS, B, B), BF16),
            pltpu.VMEM((ROWS, B, LANES), BF16),
            pltpu.VMEM((ROWS, LANES), F32),
            pltpu.VMEM((2, ROWS, LANES), F32),
            pltpu.VMEM((PAIRS, 3, B, LANES), BF16),
            pltpu.VMEM((2, PAIRS, 3, B, LANES), BF16),
            pltpu.VMEM((ROWS, B, 2 * LANES), BF16),
            pltpu.VMEM((2 * PAIRS, 3, B, LANES), BF16),
            pltpu.VMEM((2, 2 * PAIRS, 3, B, LANES), BF16),
            pltpu.VMEM((14, B, 2 * LANES), BF16),
            pltpu.VMEM((2, 2 * LANES, 2 * LANES), F32),
            pltpu.VMEM(share, BF16),
            pltpu.VMEM(share, BF16),
            pltpu.VMEM(share, BF16),
            pltpu.VMEM(share, BF16),
            pltpu.VMEM(share, BF16),
            pltpu.VMEM(share, BF16),
            pltpu.VMEM(share, F32),
            pltpu.VMEM(share, F32),
            pltpu.VMEM((PLANES * 16, LANES), F32),
            pltpu.VMEM((8, LANES), jnp.int32),
            pltpu.VMEM((PEERS, 8, LANES), jnp.int32),
            pltpu.VMEM((CHUNKS, 8 * PEERS, 4 * LANES), BF16),
            pltpu.VMEM((CHUNKS, PLANES, 16, LANES), BF16),
            pltpu.VMEM((CHUNKS, PEERS, 16, LANES), BF16),
            pltpu.VMEM((8 * PEERS, 2 * LANES), F32),
            pltpu.VMEM((PEERS, 16, LANES), BF16),
            pltpu.VMEM((PLANES, 16, LANES), BF16),
            pltpu.VMEM((PLANES * 16, LANES), F32),
            dma((3, PAIRS)),
            dma((PAIRS,)),
            dma((5,)),
            pltpu.SemaphoreType.REGULAR((BITS,)),
            dma((2,)),
            dma((2,)),
            dma((2, PAIRS)),
            dma((2, PAIRS)),
            dma((2, PAIRS)),
            dma((2, PAIRS)),
            dma((3, PAIRS)),
            dma((3, PAIRS)),
            dma((2,)),
            dma((CHUNKS,)),
            dma((CHUNKS,)),
            dma((2,)),
        ],
        compiler_params=pltpu.CompilerParams(
            collective_id=0, has_side_effects=True, vmem_limit_bytes=62 * 1024 * 1024
        ),
    )(*operands)


def on_device(
    off_blocks,
    neighbour,
    active,
    diag_blocks,
    diag_inverse,
    tentative,
    aggregate,
    owner_row,
    owner_group,
):
    return galerkin(
        neighbour.T,
        active.T,
        aggregate,
        owner_row[:, 0],
        owner_group,
        off_blocks,
        diag_blocks,
        diag_inverse,
        tentative,
    ).astype(F32)


def solution(mesh):
    return jax.shard_map(
        on_device,
        mesh=mesh,
        in_specs=(
            P(("row", "col"), None, None, None),
            P(("row", "col"), None),
            P(("row", "col"), None),
            P(("row", "col"), None, None),
            P(("row", "col"), None, None),
            P(("row", "col"), None, None),
            P(("row", "col")),
            P("row", None),
            P("row"),
        ),
        out_specs=P("row", "col", None),
        check_vma=False,
    )
```

```python
import jax
import jax.numpy as jnp
from jax import lax
from jax.experimental import pallas as pl
from jax.experimental.pallas import tpu as pltpu
from jax.sharding import PartitionSpec as P

MESH = pl.DeviceIdType.MESH
F32 = jnp.float32
BF16 = jnp.bfloat16
B = 96
LANES = 128
OMEGA = 0.6
ROWS = 64
PAIRS = 16
PEERS = 64
PLANES = 48
CHUNKS = 4
WINDOW = 3
LAG = 3
DIRECT = 14
EARLY = 1
BITS = 6


def pack4(b0, b1, b2, b3):
    high = lax.broadcasted_iota(jnp.int32, b0.shape, 1) >= B
    return (
        jnp.where(high, pltpu.roll(b3, 96, 1), b0),
        jnp.where(high, pltpu.roll(b3, 64, 1), b1),
        jnp.where(high, pltpu.roll(b3, 32, 1), b2),
    )


def unpack_last(t0, t1, t2):
    lane = lax.broadcasted_iota(jnp.int32, t0.shape, 1)
    return jnp.where(
        lane < 32,
        pltpu.roll(t0, 32, 1),
        jnp.where(lane < 64, pltpu.roll(t1, 64, 1), pltpu.roll(t2, 96, 1)),
    )


def dot(a, b):
    return lax.dot_general(a, b, (((1,), (0,)), ((), ())), preferred_element_type=F32)


def plane_device(r):
    z = r // 6
    return z * 8 + lax.rem(lax.rem(r, 6) + 2 * z + 2, 8)


def galerkin_kernel(
    near_hbm,
    active_hbm,
    label_hbm,
    owner_hbm,
    group_hbm,
    off_hbm,
    diag_hbm,
    inv_hbm,
    tent_hbm,
    out_ref,
    near_smem,
    active_smem,
    label_smem,
    owner_smem,
    group_smem,
    off,
    diag,
    inv,
    tent,
    wide,
    own_label,
    near_label,
    send_label,
    got_label,
    send_t,
    near_t,
    own_p,
    send_p,
    near_p,
    rim,
    part,
    send_far,
    send_next,
    send_back,
    near_far,
    near_next,
    near_back,
    hold_next,
    hold_own,
    staging,
    send_target,
    near_target,
    onehot,
    send_plane,
    near_plane,
    total_sum,
    send_group,
    near_group,
    final,
    load_sem,
    tent_sem,
    small_sem,
    round_sem,
    label_send,
    label_recv,
    t_send,
    t_recv,
    p_send,
    p_recv,
    c_send,
    c_recv,
    target_sem,
    plane_send,
    plane_recv,
    group_sem,
):
    me = lax.axis_index("col")
    right, left, opposite = [lax.rem(me + d, 4) for d in (1, 3, 2)]
    tile = lax.axis_index("row")
    z = tile // 8
    place = lax.rem(lax.rem(tile, 8) + 32 - 2 * z - 2, 8)
    holds = place < 6
    plane = z * 6 + place

    def loads(p):
        rows = pl.ds(p * 4, 4)
        return [
            pltpu.make_async_copy(off_hbm.at[rows], off.at[rows], load_sem.at[0, p]),
            pltpu.make_async_copy(diag_hbm.at[rows], diag.at[rows], load_sem.at[1, p]),
            pltpu.make_async_copy(inv_hbm.at[rows], inv.at[rows], load_sem.at[2, p]),
        ]

    def remote(src, dst, send_sem, recv_sem, col):
        return pltpu.make_async_remote_copy(
            src_ref=src,
            dst_ref=dst,
            send_sem=send_sem,
            recv_sem=recv_sem,
            device_id={"col": col},
            device_id_type=MESH,
        )

    def along_row(src, dst, send_sem, recv_sem, target):
        return pltpu.make_async_remote_copy(
            src_ref=src,
            dst_ref=dst,
            send_sem=send_sem,
            recv_sem=recv_sem,
            device_id={"row": target},
            device_id_type=MESH,
        )

    def tent_load(p):
        rows = pl.ds(p * 4, 4)
        return pltpu.make_async_copy(tent_hbm.at[rows], tent.at[rows], tent_sem.at[p])

    small = [
        pltpu.make_async_copy(src, dst, small_sem.at[i])
        for i, (src, dst) in enumerate(
            [
                (label_hbm, label_smem),
                (near_hbm, near_smem),
                (active_hbm, active_smem),
                (owner_hbm, owner_smem),
                (group_hbm, group_smem),
            ]
        )
    ]

    def partner(b):
        size = 1 << b
        return tile + size * (1 - 2 * lax.rem(tile // size, 2))

    barrier = pltpu.get_barrier_semaphore()
    for peer in (left, right, opposite):
        pl.semaphore_signal(barrier, inc=1, device_id={"col": peer}, device_id_type=MESH)
    for b in range(BITS):
        pl.semaphore_signal(barrier, inc=1, device_id={"row": partner(b)}, device_id_type=MESH)

    for copy in small:
        copy.start()

    @pl.loop(0, PAIRS)
    def _(p):
        tent_load(p).start()

    small[0].wait()

    @pl.loop(0, ROWS)
    def _(f):
        own_label[pl.ds(f, 1), :] = jnp.full((1, LANES), label_smem[f], jnp.int32).astype(F32)

    here = lax.broadcasted_iota(jnp.int32, (ROWS, LANES), 0) == lax.broadcasted_iota(
        jnp.int32, (ROWS, LANES), 1
    )
    line = jnp.sum(jnp.where(here, own_label[...], 0.0), axis=0, keepdims=True)
    send_label[...] = jnp.broadcast_to(line, (8, LANES))

    def pack_tent(p):
        tent_load(p).wait()
        for e in range(4):
            wide[p * 4 + e, :, 0:B] = tent[p * 4 + e]
        tiles = pack4(*[wide[p * 4 + e].astype(F32) for e in range(4)])
        for t in range(3):
            send_t[p, t] = tiles[t].astype(BF16)

    @pl.loop(0, EARLY)
    def _(p):
        pack_tent(p)

    pl.semaphore_wait(barrier, 3 + BITS)

    def label_copy(side):
        return remote(
            send_label, got_label.at[side], label_send.at[side], label_recv.at[side],
            right if side == 0 else left,
        )

    def t_copy(side, p):
        return remote(
            send_t.at[p], near_t.at[side, p], t_send.at[side, p], t_recv.at[side, p],
            right if side == 0 else left,
        )

    def p_copy(side, p):
        rows = pl.ds(p * 2, 2)
        return remote(
            send_p.at[rows], near_p.at[side, rows], p_send.at[side, p], p_recv.at[side, p],
            right if side == 0 else left,
        )

    def target_copy(target):
        return along_row(
            send_target, near_target.at[tile], target_sem.at[0], target_sem.at[1], target
        )

    for side in range(2):
        label_copy(side).start()

    @pl.loop(0, PAIRS)
    def _(p):
        @pl.when(p >= EARLY)
        def _():
            pack_tent(p)

        for side in range(2):
            t_copy(side, p).start()

    @pl.loop(0, PAIRS)
    def _(p):
        for copy in loads(p):
            copy.start()

    rim[6] = jnp.zeros_like(rim[6])
    rim[13] = jnp.zeros_like(rim[13])

    for b in range(BITS):
        pl.semaphore_signal(
            round_sem.at[b], inc=1, device_id={"row": partner(b)}, device_id_type=MESH
        )
        pl.semaphore_wait(round_sem.at[b], 1)

    for copy in small[1:]:
        copy.wait()
    sub = lax.broadcasted_iota(jnp.int32, (8, LANES), 0)
    lane = lax.broadcasted_iota(jnp.int32, (8, LANES), 1)
    mine = jnp.zeros((8, LANES), jnp.int32)
    for q in range(32):
        place_of = (sub == q // 8) & (lane == lax.rem(tile, 16) * 8 + q % 8)
        mine = jnp.where(place_of, owner_smem[q] * 8 + group_smem[q], mine)
    send_target[...] = mine

    @pl.loop(0, PLANES)
    def _(d):
        target = plane_device(lax.rem(tile + d, PLANES))

        @pl.when(target != tile)
        def _():
            target_copy(target).start()

    @pl.when(holds)
    def _():
        pltpu.make_async_copy(send_target, near_target.at[tile], target_sem.at[1]).start()

    for side in range(2):
        label_copy(side).wait_recv()
        column = jnp.sum(
            jnp.where(here, got_label[side, 0:1, :], 0.0), axis=1, keepdims=True
        )
        near_label[side] = jnp.broadcast_to(column, (ROWS, LANES))

    def apply(row, near_base, own):
        total = dot(diag[row], rim[near_base + own])
        for s in range(4):
            on = active_smem[s, row]
            slot = near_smem[s, row] * on + 6 * (1 - on)
            total = total + dot(off[row, s], rim[near_base + slot])
        return total

    @pl.loop(0, PAIRS)
    def _(p):
        for side in range(2):
            t_copy(side, p).wait_recv()
        for copy in loads(p):
            copy.wait()

        def spread(e, position, block, label):
            zero = jnp.zeros_like(block)
            at = (e // 2) * 7 + position + e % 2
            rim[at, :, 0:LANES] = jnp.where(label == 0.0, block, zero).astype(BF16)
            rim[at, :, LANES : 2 * LANES] = jnp.where(label == 1.0, block, zero).astype(BF16)

        for side in range(2):
            tiles = [near_t[side, p, t].astype(F32) for t in range(3)]
            tiles.append(unpack_last(*tiles))
            for e in range(4):
                spread(e, 4 * side, tiles[e], near_label[side, pl.ds(p * 4 + e, 1), :])
        for e in range(4):
            spread(e, 2, wide[p * 4 + e].astype(F32), own_label[pl.ds(p * 4 + e, 1), :])

        for c in range(2):
            blocks = []
            for k in range(2):
                row = p * 4 + c * 2 + k
                smooth = apply(row, c * 7, 2 + k).astype(BF16)
                prolong = rim[c * 7 + 2 + k].astype(F32) - OMEGA * dot(inv[row], smooth)
                rounded = prolong.astype(BF16)
                own_p[row] = rounded
                back = rounded.astype(F32)
                blocks += [back[:, 0:LANES], back[:, LANES : 2 * LANES]]
            tiles = pack4(*blocks)
            for t in range(3):
                send_p[p * 2 + c, t] = tiles[t].astype(BF16)

        @pl.when(p < WINDOW)
        def _():
            for side in range(2):
                p_copy(side, p).start()

    @pl.when(holds)
    def _():
        pltpu.make_async_copy(near_target, near_target, target_sem.at[1]).wait()
        group = lax.broadcasted_iota(jnp.int32, (8 * PEERS, LANES), 0)
        for k in range(4):
            named = near_target[16 * k]
            for t in range(1, 16):
                named = named + near_target[16 * k + t]
            for ch in range(CHUNKS):
                onehot[ch, :, k * LANES : (k + 1) * LANES] = jnp.where(
                    group == named[ch : ch + 1, :], 1.0, 0.0
                ).astype(BF16)

    def ways(p):
        odd = p % 2
        ahead = lax.rem(me + 3 + 2 * odd, 4)
        behind = lax.rem(me + 1 + 2 * odd, 4)
        return ahead, behind

    def far_copy(p, direct=False):
        return remote(
            send_far.at[p], near_far.at[p], c_send.at[0, p], c_recv.at[0, p],
            opposite if direct else ways(p)[0],
        )

    def next_copy(p):
        return remote(
            send_next.at[p], near_next.at[p], c_send.at[1, p], c_recv.at[1, p], ways(p)[0]
        )

    def back_copy(p):
        return remote(
            send_back.at[p], near_back.at[p], c_send.at[2, p], c_recv.at[2, p], ways(p)[1]
        )

    def plane_copy(ch, r, target):
        return along_row(
            send_plane.at[ch, r], near_plane.at[ch, tile], plane_send.at[ch], plane_recv.at[ch],
            target,
        )

    def forward(p):
        far_copy(p).wait_recv()
        for t in range(3):
            send_next[p, t] = (hold_next[p, t] + near_far[p, t].astype(F32)).astype(BF16)
        next_copy(p).start()

    def finish(p, direct=False):
        next_copy(p).wait_recv()
        back_copy(p).wait_recv()
        tiles = [
            hold_own[p, t] + near_next[p, t].astype(F32) + near_back[p, t].astype(F32)
            for t in range(3)
        ]
        if direct:
            far_copy(p, True).wait_recv()
            tiles = [tiles[t] + near_far[p, t].astype(F32) for t in range(3)]
        tiles.append(unpack_last(*tiles))
        for e in range(4):
            at = (e % 2) * 8 + (p % 4) * 2 + e // 2
            staging[pl.ds(at, PLANES, stride=16), :] = tiles[e]

        def send_planes():
            ch = p // 4
            send_plane[ch] = staging[...].reshape(PLANES, 16, LANES).astype(BF16)

            @pl.loop(0, PLANES)
            def _(d):
                r = lax.rem(tile + d, PLANES)
                target = plane_device(r)

                @pl.when(target != tile)
                def _():
                    plane_copy(ch, r, target).start()

                @pl.when(target == tile)
                def _():
                    pltpu.make_async_copy(
                        send_plane.at[ch, r], near_plane.at[ch, tile], plane_recv.at[ch]
                    ).start()

        if isinstance(p, int):
            if p % 4 == 3:
                send_planes()
        else:
            pl.when(lax.rem(p, 4) == 3)(send_planes)

    def products(p, direct=False):
        for side in range(2):
            p_copy(side, p).wait_recv()
        for c in range(2):
            for side in range(2):
                tiles = [near_p[side, p * 2 + c, t] for t in range(3)]
                last = unpack_last(*[tile.astype(F32) for tile in tiles]).astype(BF16)
                tiles.append(last)
                for e in range(4):
                    lanes = slice((e % 2) * LANES, (e % 2 + 1) * LANES)
                    rim[c * 7 + 4 * side + e // 2, :, lanes] = tiles[e]
            for k in range(2):
                rim[c * 7 + 2 + k] = own_p[p * 4 + c * 2 + k]
            total = None
            for k in range(2):
                row = p * 4 + c * 2 + k
                stiff = apply(row, c * 7, 2 + k).astype(BF16)
                term = lax.dot_general(
                    rim[c * 7 + 2 + k], stiff, (((0,), (0,)), ((), ())),
                    preferred_element_type=F32,
                )
                total = term if total is None else total + term
            part[c] = total

        def share(col):
            start = pl.multiple_of((col // 2) * LANES + lax.rem(col, 2) * 48, 16)
            rows = pl.ds(start, 48)
            return pack4(
                part[0, rows, 0:LANES],
                part[0, rows, LANES : 2 * LANES],
                part[1, rows, 0:LANES],
                part[1, rows, LANES : 2 * LANES],
            )

        ahead, behind = ways(p)
        tiles = share(lax.rem(me + 2, 4))
        for t in range(3):
            send_far[p, t] = tiles[t].astype(BF16)
        far_copy(p, direct).start()
        tiles = share(behind)
        for t in range(3):
            send_back[p, t] = tiles[t].astype(BF16)
        back_copy(p).start()

        if not direct:

            @pl.when(p + WINDOW < PAIRS)
            def _():
                for side in range(2):
                    p_copy(side, p + WINDOW).start()

        tiles = share(ahead)
        for t in range(3):
            if direct:
                send_next[p, t] = tiles[t].astype(BF16)
            else:
                hold_next[p, t] = tiles[t]
        if direct:
            next_copy(p).start()
        tiles = share(me)
        for t in range(3):
            hold_own[p, t] = tiles[t]

    @pl.loop(0, DIRECT)
    def _(p):
        products(p)

        @pl.when(p >= LAG)
        def _():
            forward(p - LAG)

        @pl.when(p >= 2 * LAG)
        def _():
            finish(p - 2 * LAG)

    for p in range(DIRECT, PAIRS):
        products(p, True)
        if p - LAG < DIRECT:
            forward(p - LAG)
        finish(p - 2 * LAG)
    for p in range(PAIRS - LAG, DIRECT):
        forward(p)
    for p in range(PAIRS - 2 * LAG, PAIRS):
        finish(p, p >= DIRECT)

    def group_copy(target):
        return along_row(
            send_group.at[target], near_group.at[plane], group_sem.at[0], group_sem.at[1], target
        )

    @pl.when(holds)
    def _():
        for ch in range(CHUNKS):
            here = near_plane.at[ch]
            pltpu.make_async_copy(here, here, plane_recv.at[ch]).wait()
            rows = near_plane[ch].astype(F32)
            both = [rows[:, c * 8 : c * 8 + 8, :].reshape(8 * PEERS, LANES) for c in range(2)]
            block = jnp.concatenate(both, axis=1).astype(BF16)
            term = dot(onehot[ch], block)
            total_sum[...] = term if ch == 0 else total_sum[...] + term
        both = [
            total_sum[:, c * LANES : (c + 1) * LANES].reshape(PEERS, 8, LANES) for c in range(2)
        ]
        send_group[...] = jnp.concatenate(both, axis=1).astype(BF16)

        @pl.loop(0, PEERS)
        def _(d):
            target = lax.rem(tile + d, PEERS)

            @pl.when(target != tile)
            def _():
                group_copy(target).start()

            @pl.when(target == tile)
            def _():
                pltpu.make_async_copy(
                    send_group.at[tile], near_group.at[plane], group_sem.at[1]
                ).start()

    for side in range(2):
        label_copy(side).wait_send()

    @pl.loop(0, PAIRS)
    def _(p):
        for side in range(2):
            t_copy(side, p).wait_send()
            p_copy(side, p).wait_send()
        far_copy(p).wait_send()
        next_copy(p).wait_send()
        back_copy(p).wait_send()

    @pl.loop(0, PLANES)
    def _(r):
        target = plane_device(r)

        @pl.when(target != tile)
        def _():
            target_copy(target).wait_send()
            for ch in range(CHUNKS):
                plane_copy(ch, r, target).wait_send()

    pltpu.make_async_copy(near_group, near_group, group_sem.at[1]).wait()
    final[...] = near_group[...].astype(F32).reshape(PLANES * 16, LANES)
    for g in range(8):
        first = final[pl.ds(g, PLANES, stride=16), :]
        second = pltpu.roll(final[pl.ds(8 + g, PLANES, stride=16), :], 96, 1)
        high = lax.broadcasted_iota(jnp.int32, first.shape, 1) >= B
        out_ref[g, :, 0:LANES] = jnp.where(high, second, first).astype(BF16)
        out_ref[g, :, LANES : 2 * B] = second[:, 0 : 2 * B - LANES].astype(BF16)

    @pl.when(holds)
    def _():
        @pl.loop(1, PEERS)
        def _(d):
            group_copy(lax.rem(tile + d, PEERS)).wait_send()


def galerkin(*operands):
    dma = pltpu.SemaphoreType.DMA
    hbm = pl.BlockSpec(memory_space=pltpu.HBM)
    share = (PAIRS, 3, 48, LANES)
    return pl.pallas_call(
        galerkin_kernel,
        out_shape=jax.ShapeDtypeStruct((8, PLANES, 2 * B), BF16),
        in_specs=[hbm] * 9,
        out_specs=pl.BlockSpec(memory_space=pltpu.VMEM),
        scratch_shapes=[
            pltpu.SMEM((4, ROWS), jnp.int32),
            pltpu.SMEM((4, ROWS), jnp.int32),
            pltpu.SMEM((ROWS,), jnp.int32),
            pltpu.SMEM((32,), jnp.int32),
            pltpu.SMEM((32,), jnp.int32),
            pltpu.VMEM((ROWS, 4, B, B), BF16),
            pltpu.VMEM((ROWS, B, B), BF16),
            pltpu.VMEM((ROWS, B, B), BF16),
            pltpu.VMEM((ROWS, B, B), BF16),
            pltpu.VMEM((ROWS, B, LANES), BF16),
            pltpu.VMEM((ROWS, LANES), F32),
            pltpu.VMEM((2, ROWS, LANES), F32),
            pltpu.VMEM((8, LANES), F32),
            pltpu.VMEM((2, 8, LANES), F32),
            pltpu.VMEM((PAIRS, 3, B, LANES), BF16),
            pltpu.VMEM((2, PAIRS, 3, B, LANES), BF16),
            pltpu.VMEM((ROWS, B, 2 * LANES), BF16),
            pltpu.VMEM((2 * PAIRS, 3, B, LANES), BF16),
            pltpu.VMEM((2, 2 * PAIRS, 3, B, LANES), BF16),
            pltpu.VMEM((14, B, 2 * LANES), BF16),
            pltpu.VMEM((2, 2 * LANES, 2 * LANES), F32),
            pltpu.VMEM(share, BF16),
            pltpu.VMEM(share, BF16),
            pltpu.VMEM(share, BF16),
            pltpu.VMEM(share, BF16),
            pltpu.VMEM(share, BF16),
            pltpu.VMEM(share, BF16),
            pltpu.VMEM(share, F32),
            pltpu.VMEM(share, F32),
            pltpu.VMEM((PLANES * 16, LANES), F32),
            pltpu.VMEM((8, LANES), jnp.int32),
            pltpu.VMEM((PEERS, 8, LANES), jnp.int32),
            pltpu.VMEM((CHUNKS, 8 * PEERS, 4 * LANES), BF16),
            pltpu.VMEM((CHUNKS, PLANES, 16, LANES), BF16),
            pltpu.VMEM((CHUNKS, PEERS, 16, LANES), BF16),
            pltpu.VMEM((8 * PEERS, 2 * LANES), F32),
            pltpu.VMEM((PEERS, 16, LANES), BF16),
            pltpu.VMEM((PLANES, 16, LANES), BF16),
            pltpu.VMEM((PLANES * 16, LANES), F32),
            dma((3, PAIRS)),
            dma((PAIRS,)),
            dma((5,)),
            pltpu.SemaphoreType.REGULAR((BITS,)),
            dma((2,)),
            dma((2,)),
            dma((2, PAIRS)),
            dma((2, PAIRS)),
            dma((2, PAIRS)),
            dma((2, PAIRS)),
            dma((3, PAIRS)),
            dma((3, PAIRS)),
            dma((2,)),
            dma((CHUNKS,)),
            dma((CHUNKS,)),
            dma((2,)),
        ],
        compiler_params=pltpu.CompilerParams(
            collective_id=0, has_side_effects=True, vmem_limit_bytes=62 * 1024 * 1024
        ),
    )(*operands)


def on_device(
    off_blocks,
    neighbour,
    active,
    diag_blocks,
    diag_inverse,
    tentative,
    aggregate,
    owner_row,
    owner_group,
):
    return galerkin(
        neighbour.T,
        active.T,
        aggregate,
        owner_row[:, 0],
        owner_group,
        off_blocks,
        diag_blocks,
        diag_inverse,
        tentative,
    ).astype(F32)


def solution(mesh):
    return jax.shard_map(
        on_device,
        mesh=mesh,
        in_specs=(
            P(("row", "col"), None, None, None),
            P(("row", "col"), None),
            P(("row", "col"), None),
            P(("row", "col"), None, None),
            P(("row", "col"), None, None),
            P(("row", "col"), None, None),
            P(("row", "col")),
            P("row", None),
            P("row"),
        ),
        out_specs=P("row", "col", None),
        check_vma=False,
    )
```
